256 devices in a mesh: seq: 32 (over x, z_lo, core), chan: 8 (over y, z_hi).
Axes of the slice: x: 4, y: 4, z: 8 (z_hi: 2, z_lo: 4; z = z_hi * 4 + z_lo), core: 2. Of those that a mesh axis runs over, the one named last changes fastest.
Arguments:
- gate_act: bfloat16 [1920, 16384], P('chan', 'seq'), may hold values from -3 to 3
- key_act: bfloat16 [1920, 16384], P('chan', 'seq'), may hold values from -6 to 6
- value_act: bfloat16 [1920, 16384], P('chan', 'seq'), may hold values from -6 to 6
- filter_raw: float32 [1920, 16384], P('chan', 'seq'), may hold values from -6 to 6
- decay_rate: float32 [1920], P('chan'), as said below
- out_weight: bfloat16 [1920, 1920], P('chan'), may hold values from -0.125 to 0.125
- out_grad: bfloat16 [1920, 16384], P('chan', 'seq'), may hold values from -6 to 6
Outputs:
- gate_grad: bfloat16 [1920, 16384], P('chan', 'seq')
- key_grad: bfloat16 [1920, 16384], P('chan', 'seq')
- value_grad: bfloat16 [1920, 16384], P('chan', 'seq')
- filter_grad: float32 [1920, 16384], P('chan', 'seq')
- weight_grad: float32 [1920, 1920], P('chan', 'seq')
The draws below stay inside these ranges and needn't reach their ends.
Inputs may be any that keep to these rules, and one draw needn't show every extreme that they name: `decay_rate`: rates are positive and at most 1/30 per position.
All inputs are finite; a program needn't handle non-finite values.
Results may differ from the reference program's by a relative error of at most 0.0045.
Values may be sent and summed in bfloat16 or wider, within the bound.
A program may use at most 128 MiB of HBM per device.

```python
import math
import jax
import jax.numpy as jnp

D = 1920
TOKENS = 16384


def draw_decay_rate(key, part):
    key = jax.random.fold_in(key, 11)
    key_fast, key_slow, key_pick = jax.random.split(key, 3)
    fast_rate = jnp.exp(jax.random.uniform(key_fast, (D,), jnp.float32, math.log(1.0 / 50.0), math.log(1.0 / 30.0)))
    slow_rate = jnp.exp(jax.random.uniform(key_slow, (D,), jnp.float32, math.log(0.25 / TOKENS), math.log(4.0 / TOKENS)))
    fast_share = 0.5
    chosen = jax.random.uniform(key_pick, (D,), jnp.float32) < fast_share
    return jnp.where(chosen, fast_rate, slow_rate).astype(jnp.float32)


def block_scale(own_key, extent, cuts, smallest, high):
    gain = 1.0
    for dim, blocks in cuts:
        heights = jax.random.uniform(jax.random.fold_in(jax.random.fold_in(own_key, 6), dim), (blocks,), jnp.float32, smallest / len(cuts), high / len(cuts))
        gain = gain * jnp.repeat(jnp.exp(heights), extent[dim] // blocks).reshape((-1,) + (1,) * (len(extent) - 1 - dim))
    return gain


def bell_draw(stream_key, shape, scale, most, cuts=(), kind=jnp.bfloat16):
    drawn = scale * jax.random.normal(stream_key, shape, jnp.float32)
    if cuts:
        drawn = drawn * block_scale(stream_key, shape, cuts, -0.22, 0.18)
    return jnp.clip(drawn, -most, most).astype(kind)


def setup_inputs(seed: int = 0) -> dict:
    streams_of = jax.random.split(jax.random.key(seed), 8)
    gate_act = bell_draw(streams_of[0], (D, TOKENS), 0.5, 3.0, ((0, 8), (1, 32)))
    key_act = bell_draw(streams_of[1], (D, TOKENS), 1.0, 6.0, ((0, 8), (1, 32)))
    value_act = bell_draw(streams_of[2], (D, TOKENS), 1.0, 6.0, ((0, 8), (1, 32)))
    filter_raw = bell_draw(streams_of[3], (D, TOKENS), 1.0, 6.0, ((0, 8), (1, 32)), jnp.float32)
    decay_rate = draw_decay_rate(jax.random.fold_in(streams_of[7], 71), 0)
    out_weight = bell_draw(streams_of[5], (D, D), D ** -0.5, 0.125, ((0, 8),))
    out_grad = bell_draw(streams_of[6], (D, TOKENS), 1.0, 6.0, ((0, 8), (1, 32)))
    return {"gate_act": gate_act, "key_act": key_act, "value_act": value_act, "filter_raw": filter_raw, "decay_rate": decay_rate, "out_weight": out_weight, "out_grad": out_grad}


def reference(gate_act, key_act, value_act, filter_raw, decay_rate, out_weight, out_grad):
    position = jnp.arange(TOKENS, dtype=jnp.float32)
    envelope = jnp.sqrt(1.0 - jnp.exp(-2.0 * decay_rate))[None, :] * jnp.exp(-decay_rate[None, :] * position[:, None])
    kernel = filter_raw.T * envelope
    gate_full = gate_act.T.astype(jnp.float32)
    key_full = key_act.T.astype(jnp.float32)
    value_full = value_act.T.astype(jnp.float32)
    grad_rows = out_grad.T
    signal = key_full * value_full
    padded = 2 * TOKENS
    kernel_spec = jnp.fft.rfft(kernel, n=padded, axis=0)
    signal_spec = jnp.fft.rfft(signal, n=padded, axis=0)
    conv = jnp.fft.irfft(kernel_spec * signal_spec, n=padded, axis=0)[:TOKENS].astype(jnp.float32)
    gated = (gate_full * conv).astype(jnp.bfloat16)
    upstream = jnp.dot(grad_rows, out_weight.T, preferred_element_type=jnp.float32)
    weight_grad = jnp.dot(gated.T, grad_rows, preferred_element_type=jnp.float32)
    gate_grad = (upstream * conv).astype(jnp.bfloat16)
    conv_grad = upstream * gate_full
    grad_spec = jnp.fft.rfft(conv_grad, n=padded, axis=0)
    signal_grad = jnp.fft.irfft(jnp.conj(kernel_spec) * grad_spec, n=padded, axis=0)[:TOKENS].astype(jnp.float32)
    kernel_grad = jnp.fft.irfft(jnp.conj(signal_spec) * grad_spec, n=padded, axis=0)[:TOKENS].astype(jnp.float32)
    key_grad = (signal_grad * value_full).astype(jnp.bfloat16)
    value_grad = (signal_grad * key_full).astype(jnp.bfloat16)
    filter_grad = kernel_grad * envelope
    return (gate_grad.T, key_grad.T, value_grad.T, filter_grad.T, weight_grad)
```

```python
import functools
import math

import jax
import jax.numpy as jnp
import numpy as np
from jax import lax
from jax.experimental import pallas as pl
from jax.experimental.pallas import tpu as pltpu
from jax.sharding import PartitionSpec as P

F32 = jnp.float32
BF16 = jnp.bfloat16
SIDE = 128
LENGTH = SIDE * SIDE
OWNED = 8


def halves(table):
    high = np.asarray(table, np.float32).astype(jnp.bfloat16)
    low = (np.asarray(table, np.float64) - high.astype(np.float64)).astype(np.float32).astype(jnp.bfloat16)
    return high, low


def make_tables():
    n = np.arange(SIDE, dtype=np.float64)
    outer = 2.0 * np.pi * np.outer(n + 0.25, n) / SIDE
    first = np.concatenate([np.cos(outer), -np.sin(outer)], 0)
    first_high, first_low = halves(first)
    first_both = np.concatenate([first_high, first_low], 1)
    turn = 2.0 * np.pi * np.outer(n + 0.25, n) / LENGTH
    twist = np.stack([np.cos(turn), np.sin(turn)]).astype(np.float32)
    inner = 2.0 * np.pi * np.outer(n, n) / SIDE
    cosine, sine = np.cos(inner), np.sin(inner)
    forward = np.concatenate([np.concatenate([cosine, -sine], 1), np.concatenate([sine, cosine], 1)], 0)
    backward = np.concatenate([np.concatenate([cosine, sine], 1), np.concatenate([-sine, cosine], 1)], 0)
    last = np.concatenate([np.cos(outer.T), -np.sin(outer.T)], 1) / LENGTH
    return (
        first_both,
        twist,
        np.stack(halves(forward)),
        np.stack(halves(backward)),
        np.stack(halves(last)),
    )


def dot(a, b):
    return jnp.dot(a, b, preferred_element_type=F32)


def split(x):
    high = x.astype(BF16)
    return high, (x - high.astype(F32)).astype(BF16)


def forward_pair(x, first, twist, forward, count):
    a = dot(first[...], jnp.concatenate([x, x], 0))
    cosine, sine = twist[0], twist[1]
    rows = []
    for i in range(count):
        real = a[:SIDE, i * SIDE : (i + 1) * SIDE]
        imag = a[SIDE:, i * SIDE : (i + 1) * SIDE]
        rows.append(jnp.concatenate([real * cosine + imag * sine, imag * cosine - real * sine], 1))
    high, low = split(jnp.concatenate(rows, 0))
    return dot(high, forward[0]) + dot(high, forward[1]) + dot(low, forward[0])


def backward_pair(spec, twist, backward, last, count):
    high, low = split(spec)
    d = dot(high, backward[0]) + dot(high, backward[1]) + dot(low, backward[0])
    cosine, sine = twist[0], twist[1]
    columns = []
    for i in range(count):
        real = d[i * SIDE : (i + 1) * SIDE, :SIDE]
        imag = d[i * SIDE : (i + 1) * SIDE, SIDE:]
        columns.append(jnp.concatenate([real * cosine - imag * sine, imag * cosine + real * sine], 0))
    high, low = split(jnp.concatenate(columns, 1))
    return dot(last[0], high) + dot(last[1], high) + dot(last[0], low)


def product(a, b):
    ar, ai, br, bi = a[:, :SIDE], a[:, SIDE:], b[:, :SIDE], b[:, SIDE:]
    return jnp.concatenate([ar * br - ai * bi, ar * bi + ai * br], 1)


def product_conj(a, b):
    ar, ai, br, bi = a[:, :SIDE], a[:, SIDE:], b[:, :SIDE], b[:, SIDE:]
    return jnp.concatenate([ar * br + ai * bi, ar * bi - ai * br], 1)


def transform_kernel(sig, ker, gr, first, twist, forward, backward, last, conv, sgrad, kgrad):
    for c in range(OWNED):
        x = jnp.concatenate([sig[c], ker[c]], 1)
        spec = forward_pair(x, first, twist, forward, 2)
        sspec, kspec = spec[:SIDE], spec[SIDE:]
        conv[c] = backward_pair(product(sspec, kspec), twist, backward, last, 1).astype(BF16)
        gspec = forward_pair(gr[c], first, twist, forward, 1)
        both = jnp.concatenate([product_conj(kspec, gspec), product_conj(sspec, gspec)], 0)
        y = backward_pair(both, twist, backward, last, 2)
        sgrad[c] = y[:, :SIDE].astype(BF16)
        kgrad[c] = y[:, SIDE:].astype(BF16)


def convolve(sig, ker, gr):
    tables = [jnp.asarray(t) for t in make_tables()]
    shape = jax.ShapeDtypeStruct((OWNED, SIDE, SIDE), BF16)
    return pl.pallas_call(
        transform_kernel,
        out_shape=(shape,) * 3,
        compiler_params=pltpu.CompilerParams(vmem_limit_bytes=32 * 2**20),
    )(sig, ker, gr, *tables)


def gather_rows(x):
    pieces = lax.axis_size("seq")
    channels, length = x.shape
    x = jnp.pad(x, ((0, OWNED * pieces - channels), (0, 0)))
    y = lax.all_to_all(x.reshape(pieces, OWNED, length), "seq", split_axis=0, concat_axis=0, tiled=True)
    return y.reshape(pieces, OWNED, length // SIDE, SIDE).transpose(1, 0, 2, 3).reshape(OWNED, SIDE, SIDE)


def scatter_rows(y, channels, length):
    pieces = lax.axis_size("seq")
    x = y.reshape(OWNED, pieces, length // SIDE, SIDE).transpose(1, 0, 2, 3).reshape(pieces, OWNED, length)
    x = lax.all_to_all(x, "seq", split_axis=0, concat_axis=0, tiled=True)
    return x.reshape(pieces * OWNED, length)[:channels].astype(F32)


def per_device(gate_act, key_act, value_act, filter_raw, decay_rate, out_weight, out_grad):
    channels, length = gate_act.shape
    device_index = lax.axis_index("seq")
    position = (device_index * length + lax.iota(jnp.int32, length)).astype(F32)
    envelope = jnp.sqrt(1.0 - jnp.exp(-2.0 * decay_rate))[:, None] * jnp.exp(
        -decay_rate[:, None] * position[None, :]
    )
    kernel = (filter_raw * envelope).astype(BF16)
    gate_full = gate_act.astype(F32)
    key_full = key_act.astype(F32)
    value_full = value_act.astype(F32)
    signal = (key_full * value_full).astype(BF16)
    everything = lax.all_gather(out_grad, "chan", axis=0, tiled=True)
    sig = gather_rows(signal)
    ker = gather_rows(kernel)
    upstream = jnp.dot(out_weight, everything, preferred_element_type=F32)
    gr = gather_rows((upstream * gate_full).astype(BF16))
    conv, sgrad, kgrad = convolve(sig, ker, gr)
    conv = scatter_rows(conv, channels, length)
    sgrad = scatter_rows(sgrad, channels, length)
    kgrad = scatter_rows(kgrad, channels, length)
    gated = (gate_full * conv).astype(BF16)
    partial = lax.dot_general(gated, everything, (((1,), (1,)), ((), ())), preferred_element_type=F32)
    pieces = lax.axis_size("seq")
    partial = partial.reshape(channels, pieces, -1).transpose(1, 0, 2)
    weight_grad = lax.psum_scatter(partial, "seq", scatter_dimension=0, tiled=False)
    return (
        (upstream * conv).astype(BF16),
        (sgrad * value_full).astype(BF16),
        (sgrad * key_full).astype(BF16),
        kgrad * envelope,
        weight_grad,
    )


def solution(mesh):
    rows = P("chan", "seq")
    return jax.shard_map(
        per_device,
        mesh=mesh,
        in_specs=(rows, rows, rows, rows, P("chan"), P("chan", None), rows),
        out_specs=(rows,) * 5,
        check_vma=False,
    )
```

```python
import functools
import math

import jax
import jax.numpy as jnp
import numpy as np
from jax import lax
from jax.experimental import pallas as pl
from jax.experimental.pallas import tpu as pltpu
from jax.sharding import PartitionSpec as P

F32 = jnp.float32
BF16 = jnp.bfloat16
SIDE = 128
LENGTH = SIDE * SIDE
OWNED = 8
PIECES = 32
GROUPS = 8
HALF = 256


def halves(table):
    high = np.asarray(table, np.float32).astype(jnp.bfloat16)
    low = (np.asarray(table, np.float64) - high.astype(np.float64)).astype(np.float32).astype(jnp.bfloat16)
    return high, low


def make_tables():
    n = np.arange(SIDE, dtype=np.float64)
    outer = 2.0 * np.pi * np.outer(n + 0.25, n) / SIDE
    first = np.concatenate([np.cos(outer), -np.sin(outer)], 0)
    first_high, first_low = halves(first)
    first_both = np.concatenate([first_high, first_low], 1)
    turn = 2.0 * np.pi * np.outer(n + 0.25, n) / LENGTH
    twist = np.stack([np.cos(turn), np.sin(turn)]).astype(np.float32)
    inner = 2.0 * np.pi * np.outer(n, n) / SIDE
    cosine, sine = np.cos(inner), np.sin(inner)
    forward = np.concatenate([np.concatenate([cosine, -sine], 1), np.concatenate([sine, cosine], 1)], 0)
    backward = np.concatenate([np.concatenate([cosine, sine], 1), np.concatenate([-sine, cosine], 1)], 0)
    last = np.concatenate([np.cos(outer.T), -np.sin(outer.T)], 1) / LENGTH
    return (
        first_both,
        twist,
        np.stack(halves(forward)),
        np.stack(halves(backward)),
        np.stack(halves(last)),
    )


def dot(a, b):
    return jnp.dot(a, b, preferred_element_type=F32)


def split(x):
    high = x.astype(BF16)
    return high, (x - high.astype(F32)).astype(BF16)


def forward_pair(x, first, twist, forward, count):
    a = dot(first[...], jnp.concatenate([x, x], 0))
    cosine, sine = twist[0], twist[1]
    rows = []
    for i in range(count):
        real = a[:SIDE, i * SIDE : (i + 1) * SIDE]
        imag = a[SIDE:, i * SIDE : (i + 1) * SIDE]
        rows.append(jnp.concatenate([real * cosine + imag * sine, imag * cosine - real * sine], 1))
    high, low = split(jnp.concatenate(rows, 0))
    return dot(high, forward[0]) + dot(high, forward[1]) + dot(low, forward[0])


def backward_pair(spec, twist, backward, last, count):
    high, low = split(spec)
    d = dot(high, backward[0]) + dot(high, backward[1]) + dot(low, backward[0])
    cosine, sine = twist[0], twist[1]
    columns = []
    for i in range(count):
        real = d[i * SIDE : (i + 1) * SIDE, :SIDE]
        imag = d[i * SIDE : (i + 1) * SIDE, SIDE:]
        columns.append(jnp.concatenate([real * cosine - imag * sine, imag * cosine + real * sine], 0))
    high, low = split(jnp.concatenate(columns, 1))
    return dot(last[0], high) + dot(last[1], high) + dot(last[0], low)


def product(a, b):
    ar, ai, br, bi = a[:, :SIDE], a[:, SIDE:], b[:, :SIDE], b[:, SIDE:]
    return jnp.concatenate([ar * br - ai * bi, ar * bi + ai * br], 1)


def product_conj(a, b):
    ar, ai, br, bi = a[:, :SIDE], a[:, SIDE:], b[:, :SIDE], b[:, SIDE:]
    return jnp.concatenate([ar * br + ai * bi, ar * bi - ai * br], 1)


def start_exchange(me, target, source, landing, send_sem, recv_sem):
    pltpu.make_async_remote_copy(
        src_ref=source.at[target],
        dst_ref=landing.at[me],
        send_sem=send_sem.at[target],
        recv_sem=recv_sem.at[me],
        device_id={"seq": target},
        device_id_type=pl.DeviceIdType.MESH,
    ).start()


def wait_arrival(origin, source, landing, send_sem, recv_sem):
    pltpu.make_async_remote_copy(
        src_ref=source.at[origin],
        dst_ref=landing.at[origin],
        send_sem=send_sem.at[origin],
        recv_sem=recv_sem.at[origin],
        device_id={"seq": origin},
        device_id_type=pl.DeviceIdType.MESH,
    ).wait_recv()


def wait_departure(target, source, landing, send_sem, recv_sem):
    pltpu.make_async_remote_copy(
        src_ref=source.at[target],
        dst_ref=landing.at[target],
        send_sem=send_sem.at[target],
        recv_sem=recv_sem.at[target],
        device_id={"seq": target},
        device_id_type=pl.DeviceIdType.MESH,
    ).wait_send()


def stacked(upper, lower):
    return jnp.concatenate([upper, lower], 0)


def beside(left, right):
    return jnp.concatenate([left, right], 1)


def whole_kernel(
    gate, key, value, filt, rate, weight, cotangent, first, twist, forward, backward, last,
    gate_grad, key_grad, value_grad, filter_grad, weight_grad,
    send1, recv1, send2, recv2, send3, recv3, send4, recv4,
    gathered, upstream, envelope, rows1, rows2, specs, out1, out2, gated,
    partial, core_in, chip_sum, x_in, x_sum, z_in,
    ss1, rs1, ss2, rs2, ss3, rs3, ss4, rs4, ag_send, ag_recv, core_send, core_recv, x_send, x_recv, z_send, z_recv,
):
    me = lax.axis_index("seq")
    group = lax.axis_index("chan")
    owners = gate.shape[0] // OWNED
    core = me % 2
    sibling = me + 1 - 2 * core
    z = (me // 2) % 4
    x = me // 8
    far = group + 1 - 2 * (group % 2)
    pairs = owners // 2
    blocks = gate.shape[0]
    owner = me < owners
    MESH = pl.DeviceIdType.MESH

    barrier = pltpu.get_barrier_semaphore()

    @pl.loop(1, PIECES)
    def _(k):
        pl.semaphore_signal(barrier, inc=1, device_id={"seq": (me + k) % PIECES}, device_id_type=MESH)

    for k in (1, 2, 3):
        pl.semaphore_signal(barrier, inc=1, device_id={"chan": (group + 2 * k) % GROUPS}, device_id_type=MESH)
    pl.semaphore_signal(barrier, inc=1, device_id={"chan": far}, device_id_type=MESH)

    gathered[pl.ds(pl.multiple_of(blocks * group, 16), blocks), :] = cotangent[...]
    gathered[pl.ds(blocks * GROUPS, 16), :] = jnp.zeros((16, gathered.shape[1]), BF16)
    gated[pl.ds(blocks, 16), :] = jnp.zeros((16, gated.shape[1]), BF16)

    position = (me * gate.shape[1] + lax.broadcasted_iota(jnp.int32, (16, gate.shape[1]), 1)).astype(F32)

    @pl.loop(0, pairs)
    def _(p):
        r = pl.ds(pl.multiple_of(16 * p, 16), 16)
        sig = key[r, :].astype(F32) * value[r, :].astype(F32)
        speed = rate[r, :]
        window = jnp.sqrt(1.0 - jnp.exp(-2.0 * speed)) * jnp.exp(-speed * position)
        envelope[r, :] = window
        ker = filt[r, :] * window
        send1[2 * p] = stacked(sig[:8], ker[:8]).astype(BF16)
        send1[2 * p + 1] = stacked(sig[8:], ker[8:]).astype(BF16)

    pl.semaphore_wait(barrier, PIECES - 1 + 4)

    def gather_copy(index, slot, target):
        rows = gathered.at[pl.ds(pl.multiple_of(blocks * slot, 16), blocks)]
        return pltpu.make_async_remote_copy(
            src_ref=rows,
            dst_ref=rows,
            send_sem=ag_send.at[index],
            recv_sem=ag_recv.at[slot],
            device_id={"chan": target},
            device_id_type=MESH,
        )

    gather_copy(0, group, far).start()
    for k in (1, 2, 3):
        gather_copy(k, group, (group + 2 * k) % GROUPS).start()

    def to_owners(source, landing, send_sem, recv_sem):
        @pl.loop(1, PIECES)
        def _(k):
            target = (me + k) % PIECES

            @pl.when(target < owners)
            def _():
                start_exchange(me, target, source, landing, send_sem, recv_sem)

        @pl.when(owner)
        def _():
            landing[me] = source[me]

    to_owners(send1, recv1, ss1, rs1)

    gather_copy(0, far, far).wait_recv()
    for k in (1, 2, 3):
        gather_copy(3 + k, far, (group + 2 * k) % GROUPS).start()

    @pl.when(owner)
    def _():
        @pl.loop(0, PIECES)
        def _(s):
            @pl.when(s != me)
            def _():
                wait_arrival(s, send1, recv1, ss1, rs1)

            piece = recv1[s].astype(F32)
            for i in range(4):
                rows1[pl.ds(pl.multiple_of((s * 4 + i) * 16, 16), 16), :] = piece[:, i * SIDE : (i + 1) * SIDE]

        @pl.loop(0, OWNED)
        def _(c):
            sig = rows1[pl.ds(c, SIDE, stride=16), :]
            ker = rows1[pl.ds(c + 8, SIDE, stride=16), :]
            spec = forward_pair(beside(sig, ker).astype(BF16), first, twist, forward, 2)
            specs[c] = spec
            out1[pl.ds(c, SIDE, stride=8), :] = backward_pair(
                product(spec[:SIDE], spec[SIDE:]), twist, backward, last, 1
            )

        @pl.loop(0, PIECES)
        def _(k):
            s = (me + k) % PIECES
            t = [out1[pl.ds(pl.multiple_of((s * 4 + i) * 8, 8), 8), :] for i in range(4)]
            send3[s] = beside(stacked(t[0], t[2]), stacked(t[1], t[3])).astype(BF16)

            @pl.when(k > 0)
            def _():
                start_exchange(me, s, send3, recv3, ss3, rs3)

            @pl.when(k == 0)
            def _():
                recv3[me] = send3[me]

    for k in (1, 2, 3):
        near = (group + 2 * k) % GROUPS
        gather_copy(0, near, near).wait_recv()
        other = near + 1 - 2 * (near % 2)
        gather_copy(0, other, near).wait_recv()
    depth = blocks * GROUPS
    for n in range(gate.shape[1] // HALF):
        cols = pl.ds(n * HALF, HALF)
        upstream[:, cols] = dot(weight[...], gathered[pl.ds(0, depth), cols])

    @pl.loop(0, pairs)
    def _(p):
        r = pl.ds(pl.multiple_of(16 * p, 16), 16)
        g = upstream[r, :] * gate[r, :].astype(F32)
        send2[2 * p] = stacked(g[:8, :HALF], g[:8, HALF:]).astype(BF16)
        send2[2 * p + 1] = stacked(g[8:, :HALF], g[8:, HALF:]).astype(BF16)

    to_owners(send2, recv2, ss2, rs2)

    @pl.loop(0, pairs)
    def _(p):
        r = pl.ds(pl.multiple_of(16 * p, 16), 16)
        for e in range(2):
            @pl.when(2 * p + e != me)
            def _():
                wait_arrival(2 * p + e, send3, recv3, ss3, rs3)

        a = recv3[2 * p].astype(F32)
        b = recv3[2 * p + 1].astype(F32)
        conv = stacked(beside(a[:8], a[8:]), beside(b[:8], b[8:]))
        gate_grad[r, :] = (upstream[r, :] * conv).astype(BF16)
        gated[r, :] = (gate[r, :].astype(F32) * conv).astype(BF16)

    for j in range(GROUPS):
        term = lax.dot_general(
            gathered[pl.ds(blocks * j, HALF), :], gated[...], (((1,), (1,)), ((), ())), preferred_element_type=F32
        )
        for g in range(4):
            partial[g % 2, 2 * j + g // 2] = term[60 * g : 60 * g + 64]

    core_copy = pltpu.make_async_remote_copy(
        src_ref=partial.at[1 - core],
        dst_ref=core_in,
        send_sem=core_send,
        recv_sem=core_recv,
        device_id={"seq": sibling},
        device_id_type=MESH,
    )
    core_copy.start()

    @pl.when(owner)
    def _():
        @pl.loop(0, PIECES)
        def _(s):
            @pl.when(s != me)
            def _():
                wait_arrival(s, send2, recv2, ss2, rs2)

            piece = recv2[s].astype(F32)
            for i in range(4):
                h, l = i // 2, i % 2
                rows2[pl.ds(pl.multiple_of((s * 4 + i) * 8, 8), 8), :] = piece[
                    h * 8 : h * 8 + 8, l * SIDE : (l + 1) * SIDE
                ]

    core_copy.wait_recv()
    chip_sum[...] = partial[core] + core_in[...]

    def x_copy(k):
        there = (x + k) % 4
        return pltpu.make_async_remote_copy(
            src_ref=chip_sum.at[pl.ds(4 * there, 4)],
            dst_ref=x_in.at[k - 1],
            send_sem=x_send.at[k - 1],
            recv_sem=x_recv.at[k - 1],
            device_id={"seq": (me + 8 * k) % PIECES},
            device_id_type=MESH,
        )

    for k in (1, 2, 3):
        x_copy(k).start()

    @pl.when(owner)
    def _():
        @pl.loop(0, OWNED)
        def _(c):
            g = rows2[pl.ds(c, SIDE, stride=8), :].astype(BF16)
            gspec = forward_pair(g, first, twist, forward, 1)
            spec = specs[c]
            both = stacked(product_conj(spec[SIDE:], gspec), product_conj(spec[:SIDE], gspec))
            y = backward_pair(both, twist, backward, last, 2)
            out2[pl.ds(c, SIDE, stride=16), :] = y[:, :SIDE]
            out2[pl.ds(c + 8, SIDE, stride=16), :] = y[:, SIDE:]

        @pl.loop(0, PIECES)
        def _(k):
            s = (me + k) % PIECES
            t = [out2[pl.ds(pl.multiple_of((s * 4 + i) * 16, 16), 16), :] for i in range(4)]
            send4[s] = jnp.concatenate(t, 1).astype(BF16)

            @pl.when(k > 0)
            def _():
                start_exchange(me, s, send4, recv4, ss4, rs4)

            @pl.when(k == 0)
            def _():
                recv4[me] = send4[me]

    for k in (1, 2, 3):
        x_copy(k).wait_recv()
    x_sum[...] = chip_sum[pl.ds(4 * x, 4)] + x_in[0] + x_in[1] + x_in[2]

    def z_copy(k):
        there = (z + k) % 4
        return pltpu.make_async_remote_copy(
            src_ref=x_sum.at[there],
            dst_ref=z_in.at[k - 1],
            send_sem=z_send.at[k - 1],
            recv_sem=z_recv.at[k - 1],
            device_id={"seq": x * 8 + there * 2 + core},
            device_id_type=MESH,
        )

    for k in (1, 2, 3):
        z_copy(k).start()

    @pl.loop(0, pairs)
    def _(p):
        r = pl.ds(pl.multiple_of(16 * p, 16), 16)
        for e in range(2):
            @pl.when(2 * p + e != me)
            def _():
                wait_arrival(2 * p + e, send4, recv4, ss4, rs4)

        a = recv4[2 * p].astype(F32)
        b = recv4[2 * p + 1].astype(F32)
        sgrad = stacked(a[:8], b[:8])
        kgrad = stacked(a[8:], b[8:])
        key_grad[r, :] = (sgrad * value[r, :].astype(F32)).astype(BF16)
        value_grad[r, :] = (sgrad * key[r, :].astype(F32)).astype(BF16)
        filter_grad[r, :] = kgrad * envelope[r, :]

    for k in (1, 2, 3):
        z_copy(k).wait_recv()
    total = x_sum[z] + z_in[0] + z_in[1] + z_in[2]
    turned = stacked(total, total).T
    weight_grad[...] = turned[:blocks, : weight_grad.shape[1]]

    for k in (1, 2, 3):
        x_copy(k).wait_send()
        z_copy(k).wait_send()
        gather_copy(k, group, (group + 2 * k) % GROUPS).wait_send()
        gather_copy(3 + k, far, (group + 2 * k) % GROUPS).wait_send()
    gather_copy(0, group, far).wait_send()
    core_copy.wait_send()

    @pl.loop(1, PIECES)
    def _(k):
        target = (me + k) % PIECES

        @pl.when(target < owners)
        def _():
            wait_departure(target, send1, recv1, ss1, rs1)
            wait_departure(target, send2, recv2, ss2, rs2)

        @pl.when(owner)
        def _():
            wait_departure(target, send3, recv3, ss3, rs3)
            wait_departure(target, send4, recv4, ss4, rs4)


def per_device(gate_act, key_act, value_act, filter_raw, decay_rate, out_weight, out_grad):
    channels, length = gate_act.shape
    tables = [jnp.asarray(t) for t in make_tables()]
    shape = (channels, length)
    vmem = pltpu.VMEM
    dma = pltpu.SemaphoreType.DMA
    rows = SIDE * OWNED
    return pl.pallas_call(
        whole_kernel,
        out_shape=(
            jax.ShapeDtypeStruct(shape, BF16),
            jax.ShapeDtypeStruct(shape, BF16),
            jax.ShapeDtypeStruct(shape, BF16),
            jax.ShapeDtypeStruct(shape, F32),
            jax.ShapeDtypeStruct((channels, channels * GROUPS // PIECES), F32),
        ),
        scratch_shapes=[
            vmem((PIECES, 16, length), BF16),
            vmem((PIECES, 16, length), BF16),
            vmem((PIECES, 16, HALF), BF16),
            vmem((PIECES, 16, HALF), BF16),
            vmem((PIECES, 16, HALF), BF16),
            vmem((PIECES, 16, HALF), BF16),
            vmem((PIECES, 16, length), BF16),
            vmem((PIECES, 16, length), BF16),
            vmem((channels * GROUPS + 16, length), BF16),
            vmem(shape, F32),
            vmem(shape, F32),
            vmem((2 * rows, SIDE), F32),
            vmem((rows, SIDE), F32),
            vmem((OWNED, 2 * SIDE, 2 * SIDE), F32),
            vmem((rows, SIDE), F32),
            vmem((2 * rows, SIDE), F32),
            vmem((channels + 16, length), BF16),
            vmem((2, 16, 64, HALF), F32),
            vmem((16, 64, HALF), F32),
            vmem((16, 64, HALF), F32),
            vmem((3, 4, 64, HALF), F32),
            vmem((4, 64, HALF), F32),
            vmem((3, 64, HALF), F32),
        ]
        + [dma((PIECES,))] * 8
        + [dma((7,)), dma((GROUPS,)), dma, dma, dma((3,)), dma((3,)), dma((3,)), dma((3,))],
        compiler_params=pltpu.CompilerParams(
            collective_id=0, has_side_effects=True, vmem_limit_bytes=50 * 2**20
        ),
    )(gate_act, key_act, value_act, filter_raw, decay_rate[:, None], out_weight, out_grad, *tables)


def solution(mesh):
    rows = P("chan", "seq")
    return jax.shard_map(
        per_device,
        mesh=mesh,
        in_specs=(rows, rows, rows, rows, P("chan"), P("chan", None), rows),
        out_specs=(rows,) * 5,
        check_vma=False,
    )
```

```python
import functools
import math

import jax
import jax.numpy as jnp
import numpy as np
from jax import lax
from jax.experimental import pallas as pl
from jax.experimental.pallas import tpu as pltpu
from jax.sharding import PartitionSpec as P

F32 = jnp.float32
BF16 = jnp.bfloat16
SIDE = 128
LENGTH = SIDE * SIDE
OWNED = 8
PIECES = 32
GROUPS = 8
HALF = 256
BATCH = 4
LIMIT = 63 * 2**20
CHUNKS = ((0, 64), (64, 64), (128, 64), (192, 48))
MESH = pl.DeviceIdType.MESH


def halves(table):
    high = np.asarray(table, np.float32).astype(jnp.bfloat16)
    low = (np.asarray(table, np.float64) - high.astype(np.float64)).astype(np.float32).astype(jnp.bfloat16)
    return high, low


def make_tables():
    n = np.arange(SIDE, dtype=np.float64)
    outer = 2.0 * np.pi * np.outer(n + 0.25, n) / SIDE
    first = np.concatenate([np.cos(outer), -np.sin(outer)], 0)
    first_high, first_low = halves(first)
    first_both = np.concatenate([first_high, first_low], 1)
    turn = 2.0 * np.pi * np.outer(n + 0.25, n) / LENGTH
    twist = np.stack([np.cos(turn), np.sin(turn)]).astype(np.float32)
    inner = 2.0 * np.pi * np.outer(n, n) / SIDE
    cosine, sine = np.cos(inner), np.sin(inner)
    forward = np.concatenate([np.concatenate([cosine, -sine], 1), np.concatenate([sine, cosine], 1)], 0)
    backward = np.concatenate([np.concatenate([cosine, sine], 1), np.concatenate([-sine, cosine], 1)], 0)
    last = np.concatenate([np.cos(outer.T), -np.sin(outer.T)], 1) / LENGTH
    return (
        first_both.astype(np.float32),
        twist,
        np.stack(halves(forward)).astype(np.float32),
        np.stack(halves(backward)).astype(np.float32),
        np.stack(halves(last)).astype(np.float32),
    )


def dot(a, b):
    return jnp.dot(a, b, preferred_element_type=F32)


def split(x):
    high = x.astype(BF16)
    return high, (x - high.astype(F32)).astype(BF16)


def forward_pair(x, first, twist, forward, count):
    a = dot(first[...], jnp.concatenate([x, x], 0))
    cosine, sine = twist[0], twist[1]
    rows = []
    for i in range(count):
        real = a[:SIDE, i * SIDE : (i + 1) * SIDE]
        imag = a[SIDE:, i * SIDE : (i + 1) * SIDE]
        rows.append(jnp.concatenate([real * cosine + imag * sine, imag * cosine - real * sine], 1))
    high, low = split(jnp.concatenate(rows, 0))
    return dot(jnp.concatenate([high, high, low], 1), forward[...])


def backward_pair(spec, twist, backward, last, count):
    high, low = split(spec)
    d = dot(jnp.concatenate([high, high, low], 1), backward[...])
    cosine, sine = twist[0], twist[1]
    columns = []
    for i in range(count):
        real = d[i * SIDE : (i + 1) * SIDE, :SIDE]
        imag = d[i * SIDE : (i + 1) * SIDE, SIDE:]
        columns.append(jnp.concatenate([real * cosine - imag * sine, imag * cosine + real * sine], 0))
    high, low = split(jnp.concatenate(columns, 1))
    return dot(last[...], jnp.concatenate([high, high, low], 0))


def product(a, b):
    ar, ai, br, bi = a[:, :SIDE], a[:, SIDE:], b[:, :SIDE], b[:, SIDE:]
    return jnp.concatenate([ar * br - ai * bi, ar * bi + ai * br], 1)


def product_conj(a, b):
    ar, ai, br, bi = a[:, :SIDE], a[:, SIDE:], b[:, :SIDE], b[:, SIDE:]
    return jnp.concatenate([ar * br + ai * bi, ar * bi - ai * br], 1)


def go(copy):
    copy.start()


def land(copy):
    copy.wait_recv()


def leave(copy):
    copy.wait_send()


def exchange(me, target, source, landing, send_sem, recv_sem):
    return pltpu.make_async_remote_copy(
        src_ref=source.at[target],
        dst_ref=landing.at[me],
        send_sem=send_sem.at[target],
        recv_sem=recv_sem.at[me],
        device_id={"seq": target},
        device_id_type=MESH,
    )


def arrival(origin, source, landing, send_sem, recv_sem):
    return exchange(origin, origin, source, landing, send_sem, recv_sem)


def stacked(upper, lower):
    return jnp.concatenate([upper, lower], 0)


def beside(left, right):
    return jnp.concatenate([left, right], 1)


def whole_kernel(
    gate_hbm, key_hbm, value_hbm, filt_hbm, rate_hbm, weight_hbm, cotangent_hbm,
    first_hbm, twist_hbm, forward_hbm, backward_hbm, last_hbm,
    gate_grad, key_grad, value_grad, filter_grad, weight_grad,
    gate, key, value, filt, rate, weight, first_in, twist, forward_in, backward_in, last_in,
    first, forward, backward, last,
    send1, recv1, send2, recv2, send3, recv3, send4, recv4,
    gathered, upstream, envelope, rows1, rows2, specs, out1, out2, gated,
    partial, core_in, chip_sum, x_in, x_sum, z_in, in_sem,
    ss1, rs1, ss2, rs2, ss3, rs3, ss4, rs4, ag_send, ag_recv, core_send, core_recv, x_send, x_recv, z_send, z_recv,
):
    me = lax.axis_index("seq")
    group = lax.axis_index("chan")
    blocks = gate.shape[0]
    length = gate.shape[1]
    owners = blocks // OWNED
    core = me % 2
    sibling = me + 1 - 2 * core
    z = (me // 2) % 4
    x = me // 8
    far = group + 1 - 2 * (group % 2)
    above = (group + 2) % GROUPS
    below = (group + GROUPS - 2) % GROUPS
    pairs = owners // 2
    owner = me < owners
    own_rows = pl.ds(pl.multiple_of(blocks * group, 16), blocks)

    loads = [
        pltpu.make_async_copy(a, b, in_sem.at[i])
        for i, (a, b) in enumerate(
            (
                (key_hbm, key),
                (value_hbm, value),
                (filt_hbm, filt),
                (rate_hbm, rate),
                (cotangent_hbm, gathered.at[own_rows]),
                (gate_hbm, gate),
                (first_hbm, first_in),
                (twist_hbm, twist),
                (forward_hbm, forward_in),
                (backward_hbm, backward_in),
                (last_hbm, last_in),
                (weight_hbm, weight),
            )
        )
    ]
    for load in loads:
        load.start()
    barrier = pltpu.get_barrier_semaphore()

    @pl.loop(1, PIECES)
    def _(k):
        pl.semaphore_signal(barrier, inc=1, device_id={"seq": (me + k) % PIECES}, device_id_type=MESH)

    for peer in (far, above, below):
        pl.semaphore_signal(barrier, inc=1, device_id={"chan": peer}, device_id_type=MESH)

    gathered[pl.ds(blocks * GROUPS, 16), :] = jnp.zeros((16, length), BF16)
    gated[pl.ds(blocks, 16), :] = jnp.zeros((16, 2 * length), BF16)
    position = (me * length + lax.broadcasted_iota(jnp.int32, (16, length), 1)).astype(F32)
    for load in loads[:4]:
        load.wait()

    @pl.loop(0, pairs)
    def _(p):
        r = pl.ds(pl.multiple_of(16 * p, 16), 16)
        sig = key[r, :].astype(F32) * value[r, :].astype(F32)
        speed = rate[r, :]
        window = jnp.sqrt(1.0 - jnp.exp(-2.0 * speed)) * jnp.exp(-speed * position)
        envelope[r, :] = window
        ker = filt[r, :] * window
        send1[2 * p] = stacked(sig[:8], ker[:8]).astype(BF16)
        send1[2 * p + 1] = stacked(sig[8:], ker[8:]).astype(BF16)

    loads[4].wait()
    pl.semaphore_wait(barrier, PIECES - 1 + 3)

    def gather_copy(index, slot, chunk, target):
        begin, count = CHUNKS[chunk]
        rows = gathered.at[pl.ds(pl.multiple_of(blocks * slot + begin, 16), count)]
        return pltpu.make_async_remote_copy(
            src_ref=rows,
            dst_ref=rows,
            send_sem=ag_send.at[index, chunk],
            recv_sem=ag_recv.at[slot, chunk],
            device_id={"chan": target},
            device_id_type=MESH,
        )

    span = range(len(CHUNKS))
    middle = len(CHUNKS) // 2
    above_far = above + 1 - 2 * (above % 2)
    below_far = below + 1 - 2 * (below % 2)

    def relay(index, from_below, from_above, chunk):
        if chunk < middle:
            return gather_copy(index, from_below, chunk, above)
        return gather_copy(index, from_above, chunk, below)

    def to_owners(source, landing, send_sem, recv_sem):
        @pl.loop(1, PIECES)
        def _(k):
            target = (me + k) % PIECES

            @pl.when(target < owners)
            def _():
                go(exchange(me, target, source, landing, send_sem, recv_sem))

        @pl.when(owner)
        def _():
            landing[me] = source[me]

    def pass_far(c):
        land(gather_copy(0, far, c, far))
        go(gather_copy(3, far, c, above))
        go(gather_copy(4, far, c, below))

    go(gather_copy(0, group, 0, far))
    go(gather_copy(0, group, 1, far))
    for c in span:
        go(gather_copy(1, group, c, above))
        go(gather_copy(2, group, (c + middle) % len(CHUNKS), below))
    for load in loads[5:]:
        load.wait()
    first[...] = first_in[...].astype(BF16)
    for i, part in enumerate((0, 1, 0)):
        rows = pl.ds(2 * SIDE * i, 2 * SIDE)
        forward[rows, :] = forward_in[part].astype(BF16)
        backward[rows, :] = backward_in[part].astype(BF16)
        last[:, rows] = last_in[part].astype(BF16)
    pass_far(0)
    go(gather_copy(0, group, 2, far))
    pass_far(1)
    go(gather_copy(0, group, 3, far))
    to_owners(send1, recv1, ss1, rs1)
    for c in span:
        land(relay(5, below, above, c))
        go(relay(5, below, above, c))
    pass_far(2)
    pass_far(3)
    for c in span:
        land(relay(6, below_far, above_far, c))
        go(relay(6, below_far, above_far, c))

    for c in span:
        if c < middle:
            land(gather_copy(0, above, c, above))
            land(gather_copy(0, above_far, c, above))
        else:
            land(gather_copy(0, below, c, below))
            land(gather_copy(0, below_far, c, below))
        opposite = (group + 4) % GROUPS
        land(gather_copy(0, opposite, c, above))
        land(gather_copy(0, opposite + 1 - 2 * (opposite % 2), c, above))
    depth = blocks * GROUPS
    for n in range(length // HALF):
        cols = pl.ds(n * HALF, HALF)
        upstream[:, cols] = dot(weight[...], gathered[pl.ds(0, depth), cols])

    @pl.loop(0, pairs)
    def _(p):
        r = pl.ds(pl.multiple_of(16 * p, 16), 16)
        g = upstream[r, :] * gate[r, :].astype(F32)
        send2[2 * p] = stacked(g[:8, :HALF], g[:8, HALF:]).astype(BF16)
        send2[2 * p + 1] = stacked(g[8:, :HALF], g[8:, HALF:]).astype(BF16)

    to_owners(send2, recv2, ss2, rs2)

    @pl.when(owner)
    def _():
        @pl.loop(0, PIECES)
        def _(s):
            @pl.when(s != me)
            def _():
                land(arrival(s, send1, recv1, ss1, rs1))

        @pl.loop(0, PIECES, unroll=4)
        def _(s):
            piece = recv1[s].astype(F32)
            for i in range(4):
                rows1[pl.ds(pl.multiple_of((s * 4 + i) * 16, 16), 16), :] = piece[:, i * SIDE : (i + 1) * SIDE]

        @pl.loop(0, OWNED // BATCH)
        def _(b):
            cs = [b * BATCH + i for i in range(BATCH)]
            sig = [rows1[pl.ds(c, SIDE, stride=16), :].astype(BF16) for c in cs]
            ker = [rows1[pl.ds(c + 8, SIDE, stride=16), :].astype(BF16) for c in cs]
            spec = forward_pair(jnp.concatenate(sig + ker, 1), first, twist, forward, 2 * BATCH)
            specs[b] = spec
            y = backward_pair(
                product(spec[: SIDE * BATCH], spec[SIDE * BATCH :]), twist, backward, last, BATCH
            )
            for i, c in enumerate(cs):
                out1[pl.ds(c, SIDE, stride=8), :] = y[:, i * SIDE : (i + 1) * SIDE]

        @pl.loop(0, PIECES, unroll=4)
        def _(s):
            t = [out1[pl.ds(pl.multiple_of((s * 4 + i) * 8, 8), 8), :] for i in range(4)]
            send3[s] = beside(stacked(t[0], t[2]), stacked(t[1], t[3])).astype(BF16)

        @pl.loop(1, PIECES)
        def _(k):
            go(exchange(me, (me + k) % PIECES, send3, recv3, ss3, rs3))

        recv3[me] = send3[me]

    @pl.when(owner)
    def _():
        @pl.loop(0, PIECES)
        def _(s):
            @pl.when(s != me)
            def _():
                land(arrival(s, send2, recv2, ss2, rs2))

        @pl.loop(0, PIECES, unroll=4)
        def _(s):
            piece = recv2[s].astype(F32)
            for i in range(4):
                h, l = i // 2, i % 2
                rows2[pl.ds(pl.multiple_of((s * 4 + i) * 8, 8), 8), :] = piece[
                    h * 8 : h * 8 + 8, l * SIDE : (l + 1) * SIDE
                ]

        @pl.loop(0, OWNED // BATCH)
        def _(b):
            cs = [b * BATCH + i for i in range(BATCH)]
            g = [rows2[pl.ds(c, SIDE, stride=8), :].astype(BF16) for c in cs]
            gspec = forward_pair(jnp.concatenate(g, 1), first, twist, forward, BATCH)
            spec = specs[b]
            both = stacked(
                product_conj(spec[SIDE * BATCH :], gspec), product_conj(spec[: SIDE * BATCH], gspec)
            )
            y = backward_pair(both, twist, backward, last, 2 * BATCH)
            for i in range(2 * BATCH):
                out2[pl.ds(i, SIDE, stride=8), :] = y[:, i * SIDE : (i + 1) * SIDE]

            @pl.loop(0, PIECES, unroll=4)
            def _(s):
                t = [out2[pl.ds(pl.multiple_of((s * 4 + i) * 8, 8), 8), :] for i in range(4)]
                send4[b, s] = beside(stacked(t[0], t[2]), stacked(t[1], t[3])).astype(BF16)

            @pl.loop(1, PIECES)
            def _(k):
                go(exchange(me, (me + k) % PIECES, send4.at[b], recv4.at[b], ss4.at[b], rs4.at[b]))

            recv4[b, me] = send4[b, me]

    def from_owners(source, landing, send_sem, recv_sem):
        @pl.loop(0, owners)
        def _(s):
            @pl.when(s != me)
            def _():
                land(arrival(s, source, landing, send_sem, recv_sem))

    from_owners(send3, recv3, ss3, rs3)

    @pl.loop(0, pairs)
    def _(p):
        r = pl.ds(pl.multiple_of(16 * p, 16), 16)
        a = recv3[2 * p].astype(F32)
        b = recv3[2 * p + 1].astype(F32)
        conv = stacked(beside(a[:8], a[8:]), beside(b[:8], b[8:]))
        gate_grad[r, :] = (upstream[r, :] * conv).astype(BF16)
        high, low = split(gate[r, :].astype(F32) * conv)
        gated[r, :] = beside(high, low)

    for j in range(GROUPS):
        rows = gathered[pl.ds(blocks * j, HALF), :]
        term = lax.dot_general(
            beside(rows, rows), gated[...], (((1,), (1,)), ((), ())), preferred_element_type=F32
        )
        for g in range(4):
            partial[g % 2, 2 * j + g // 2] = term[60 * g : 60 * g + 64]

    core_copy = pltpu.make_async_remote_copy(
        src_ref=partial.at[1 - core],
        dst_ref=core_in,
        send_sem=core_send,
        recv_sem=core_recv,
        device_id={"seq": sibling},
        device_id_type=MESH,
    )
    go(core_copy)

    def x_copy(k):
        there = (x + k) % 4
        return pltpu.make_async_remote_copy(
            src_ref=chip_sum.at[pl.ds(4 * there, 4)],
            dst_ref=x_in.at[k - 1],
            send_sem=x_send.at[k - 1],
            recv_sem=x_recv.at[k - 1],
            device_id={"seq": (me + 8 * k) % PIECES},
            device_id_type=MESH,
        )

    land(core_copy)
    partial[core] = partial[core] + core_in[...]
    chip_sum[...] = partial[core].astype(BF16)
    for k in (1, 2, 3):
        go(x_copy(k))

    for k in (1, 2, 3):
        land(x_copy(k))
    x_sum[...] = partial[core, pl.ds(4 * x, 4)] + x_in[0].astype(F32) + x_in[1].astype(F32) + x_in[2].astype(F32)

    def z_copy(k):
        there = (z + k) % 4
        return pltpu.make_async_remote_copy(
            src_ref=x_sum.at[there],
            dst_ref=z_in.at[k - 1],
            send_sem=z_send.at[k - 1],
            recv_sem=z_recv.at[k - 1],
            device_id={"seq": x * 8 + there * 2 + core},
            device_id_type=MESH,
        )

    for k in (1, 2, 3):
        go(z_copy(k))

    for b in range(2):
        from_owners(send4.at[b], recv4.at[b], ss4.at[b], rs4.at[b])

    @pl.loop(0, pairs)
    def _(p):
        r = pl.ds(pl.multiple_of(16 * p, 16), 16)
        parts = []
        for o in range(2):
            for b in range(2):
                a = recv4[b, 2 * p + o].astype(F32)
                parts.append(beside(a[:8], a[8:]))
        sgrad = jnp.concatenate([a[:4] for a in parts], 0)
        kgrad = jnp.concatenate([a[4:] for a in parts], 0)
        key_grad[r, :] = (sgrad * value[r, :].astype(F32)).astype(BF16)
        value_grad[r, :] = (sgrad * key[r, :].astype(F32)).astype(BF16)
        filter_grad[r, :] = kgrad * envelope[r, :]

    for k in (1, 2, 3):
        land(z_copy(k))
    total = x_sum[z] + z_in[0] + z_in[1] + z_in[2]
    weight_grad[...] = total[: weight_grad.shape[0], :blocks]

    for k in (1, 2, 3):
        leave(x_copy(k))
        leave(z_copy(k))
    leave(core_copy)
    for c in span:
        leave(gather_copy(0, group, c, far))
        leave(gather_copy(1, group, c, above))
        leave(gather_copy(2, group, c, below))
        leave(gather_copy(3, far, c, above))
        leave(gather_copy(4, far, c, below))
        leave(relay(5, below, above, c))
        leave(relay(6, below_far, above_far, c))

    @pl.loop(1, PIECES)
    def _(k):
        target = (me + k) % PIECES

        @pl.when(target < owners)
        def _():
            leave(exchange(me, target, send1, recv1, ss1, rs1))
            leave(exchange(me, target, send2, recv2, ss2, rs2))

        @pl.when(owner)
        def _():
            leave(exchange(me, target, send3, recv3, ss3, rs3))
            for b in range(2):
                leave(exchange(me, target, send4.at[b], recv4.at[b], ss4.at[b], rs4.at[b]))


def per_device(gate_act, key_act, value_act, filter_raw, decay_rate, out_weight, out_grad):
    channels, length = gate_act.shape
    tables = [jnp.asarray(t) for t in make_tables()]
    shape = (channels, length)
    vmem = pltpu.VMEM
    dma = pltpu.SemaphoreType.DMA
    rows = SIDE * OWNED
    *grads, weight_grad = pl.pallas_call(
        whole_kernel,
        out_shape=(
            jax.ShapeDtypeStruct(shape, BF16),
            jax.ShapeDtypeStruct(shape, BF16),
            jax.ShapeDtypeStruct(shape, BF16),
            jax.ShapeDtypeStruct(shape, F32),
            jax.ShapeDtypeStruct((channels * GROUPS // PIECES, channels), F32),
        ),
        in_specs=[pl.BlockSpec(memory_space=pltpu.HBM)] * 12,
        scratch_shapes=[
            vmem(shape, BF16),
            vmem(shape, BF16),
            vmem(shape, BF16),
            vmem(shape, F32),
            vmem((channels, 1), F32),
            vmem(out_weight.shape, BF16),
        ]
        + [vmem(t.shape, t.dtype) for t in tables]
        + [
            vmem((2 * SIDE, 2 * SIDE), BF16),
            vmem((6 * SIDE, 2 * SIDE), BF16),
            vmem((6 * SIDE, 2 * SIDE), BF16),
            vmem((SIDE, 6 * SIDE), BF16),
            vmem((PIECES, 16, length), BF16),
            vmem((PIECES, 16, length), BF16),
            vmem((PIECES, 16, HALF), BF16),
            vmem((PIECES, 16, HALF), BF16),
            vmem((PIECES, 16, HALF), BF16),
            vmem((PIECES, 16, HALF), BF16),
            vmem((2, PIECES, 16, HALF), BF16),
            vmem((2, PIECES, 16, HALF), BF16),
            vmem((channels * GROUPS + 16, length), BF16),
            vmem(shape, F32),
            vmem(shape, F32),
            vmem((2 * rows, SIDE), F32),
            vmem((rows, SIDE), F32),
            vmem((OWNED // BATCH, 2 * SIDE * BATCH, 2 * SIDE), F32),
            vmem((rows, SIDE), F32),
            vmem((rows, SIDE), F32),
            vmem((channels + 16, 2 * length), BF16),
            vmem((2, 16, 64, HALF), F32),
            vmem((16, 64, HALF), F32),
            vmem((16, 64, HALF), BF16),
            vmem((3, 4, 64, HALF), BF16),
            vmem((4, 64, HALF), F32),
            vmem((3, 64, HALF), F32),
            dma((12,)),
        ]
        + [dma((PIECES,))] * 6
        + [dma((2, PIECES))] * 2
        + [dma((7, len(CHUNKS))), dma((GROUPS, len(CHUNKS))), dma, dma]
        + [dma((3,))] * 4,
        compiler_params=pltpu.CompilerParams(
            collective_id=0, has_side_effects=True, vmem_limit_bytes=LIMIT
        ),
    )(gate_act, key_act, value_act, filter_raw, decay_rate[:, None], out_weight, out_grad, *tables)
    return (*grads, weight_grad.T)


def solution(mesh):
    rows = P("chan", "seq")
    return jax.shard_map(
        per_device,
        mesh=mesh,
        in_specs=(rows, rows, rows, rows, P("chan"), P("chan", None), rows),
        out_specs=(rows,) * 5,
        check_vma=False,
    )
```

```python
import functools
import math

import jax
import jax.numpy as jnp
import numpy as np
from jax import lax
from jax.experimental import pallas as pl
from jax.experimental.pallas import tpu as pltpu
from jax.sharding import PartitionSpec as P

F32 = jnp.float32
BF16 = jnp.bfloat16
SIDE = 128
LENGTH = SIDE * SIDE
OWNED = 8
PIECES = 32
GROUPS = 8
HALF = 256
BATCH = 4
LIMIT = 63 * 2**20
CHUNKS = ((0, 48), (48, 32), (80, 48), (128, 32), (160, 48), (208, 32))
FLIGHT = 3
A1POS = 0
OWNPOS = 2
MESH = pl.DeviceIdType.MESH


def halves(table):
    high = np.asarray(table, np.float32).astype(jnp.bfloat16)
    low = (np.asarray(table, np.float64) - high.astype(np.float64)).astype(np.float32).astype(jnp.bfloat16)
    return high, low


def make_tables():
    n = np.arange(SIDE, dtype=np.float64)
    outer = 2.0 * np.pi * np.outer(n + 0.25, n) / SIDE
    first = np.concatenate([np.cos(outer), -np.sin(outer)], 0)
    first_high, first_low = halves(first)
    first_both = np.concatenate([first_high, first_low], 1)
    turn = 2.0 * np.pi * np.outer(n + 0.25, n) / LENGTH
    twist = np.stack([np.cos(turn), np.sin(turn)]).astype(np.float32)
    inner = 2.0 * np.pi * np.outer(n, n) / SIDE
    cosine, sine = np.cos(inner), np.sin(inner)
    forward = np.concatenate([np.concatenate([cosine, -sine], 1), np.concatenate([sine, cosine], 1)], 0)
    backward = np.concatenate([np.concatenate([cosine, sine], 1), np.concatenate([-sine, cosine], 1)], 0)
    last = np.concatenate([np.cos(outer.T), -np.sin(outer.T)], 1) / LENGTH
    return (
        first_both.astype(np.float32),
        twist,
        np.stack(halves(forward)).astype(np.float32),
        np.stack(halves(backward)).astype(np.float32),
        np.stack(halves(last)).astype(np.float32),
    )


def dot(a, b):
    return jnp.dot(a, b, preferred_element_type=F32)


def split(x):
    high = x.astype(BF16)
    return high, (x - high.astype(F32)).astype(BF16)


def forward_pair(x, first, twist, forward, count):
    a = dot(first[...], jnp.concatenate([x, x], 0))
    cosine, sine = twist[0], twist[1]
    rows = []
    for i in range(count):
        real = a[:SIDE, i * SIDE : (i + 1) * SIDE]
        imag = a[SIDE:, i * SIDE : (i + 1) * SIDE]
        rows.append(jnp.concatenate([real * cosine + imag * sine, imag * cosine - real * sine], 1))
    high, low = split(jnp.concatenate(rows, 0))
    return dot(jnp.concatenate([high, high, low], 1), forward[...])


def backward_pair(spec, twist, backward, last, count):
    high, low = split(spec)
    d = dot(jnp.concatenate([high, high, low], 1), backward[...])
    cosine, sine = twist[0], twist[1]
    columns = []
    for i in range(count):
        real = d[i * SIDE : (i + 1) * SIDE, :SIDE]
        imag = d[i * SIDE : (i + 1) * SIDE, SIDE:]
        columns.append(jnp.concatenate([real * cosine - imag * sine, imag * cosine + real * sine], 0))
    high, low = split(jnp.concatenate(columns, 1))
    return dot(last[...], jnp.concatenate([high, high, low], 0))


def product(a, b):
    ar, ai, br, bi = a[:, :SIDE], a[:, SIDE:], b[:, :SIDE], b[:, SIDE:]
    return jnp.concatenate([ar * br - ai * bi, ar * bi + ai * br], 1)


def product_conj(a, b):
    ar, ai, br, bi = a[:, :SIDE], a[:, SIDE:], b[:, :SIDE], b[:, SIDE:]
    return jnp.concatenate([ar * br + ai * bi, ar * bi - ai * br], 1)


def go(copy):
    copy.start()


def land(copy):
    copy.wait_recv()


def leave(copy):
    copy.wait_send()


def exchange(me, target, source, landing, send_sem, recv_sem):
    return pltpu.make_async_remote_copy(
        src_ref=source.at[target],
        dst_ref=landing.at[me],
        send_sem=send_sem.at[target],
        recv_sem=recv_sem.at[me],
        device_id={"seq": target},
        device_id_type=MESH,
    )


def arrival(origin, source, landing, send_sem, recv_sem):
    return exchange(origin, origin, source, landing, send_sem, recv_sem)


def stacked(upper, lower):
    return jnp.concatenate([upper, lower], 0)


def beside(left, right):
    return jnp.concatenate([left, right], 1)


def whole_kernel(
    gate_hbm, key_hbm, value_hbm, filt_hbm, rate_hbm, weight_hbm, cotangent_hbm,
    first_hbm, twist_hbm, forward_hbm, backward_hbm, last_hbm,
    gate_grad, key_grad, value_grad, filter_grad, weight_grad,
    gate, key, value, filt, rate_in, rate, weight, first_in, twist, forward_in, backward_in, last_in,
    first, forward, backward, last,
    send1, recv1, send2, recv2, send3, recv3, send4, recv4,
    gathered, upstream, envelope, rows1, rows2, specs, out1, out2, gated,
    partial, core_in, chip_sum, x_in, x_sum, x_out, z_in, in_sem,
    ss1, rs1, ss2, rs2, ss3, rs3, ss4, rs4, ag_send, ag_recv, core_send, core_recv, x_send, x_recv, z_send, z_recv,
):
    me = lax.axis_index("seq")
    group = lax.axis_index("chan")
    blocks = gate.shape[0]
    length = gate.shape[1]
    owners = blocks // OWNED
    core = me % 2
    sibling = me + 1 - 2 * core
    z = (me // 2) % 4
    x = me // 8
    far = group + 1 - 2 * (group % 2)
    above = (group + 2) % GROUPS
    below = (group + GROUPS - 2) % GROUPS
    pairs = owners // 2
    owner = me < owners
    own_rows = pl.ds(pl.multiple_of(blocks * group, 16), blocks)

    loads = [
        pltpu.make_async_copy(a, b, in_sem.at[i])
        for i, (a, b) in enumerate(
            (
                (key_hbm, key),
                (value_hbm, value),
                (filt_hbm, filt),
                (rate_hbm, rate_in),
                (cotangent_hbm, gathered.at[own_rows]),
                (gate_hbm, gate),
                (first_hbm, first_in),
                (twist_hbm, twist),
                (forward_hbm, forward_in),
                (backward_hbm, backward_in),
                (last_hbm, last_in),
                (weight_hbm, weight),
            )
        )
    ]
    for load in loads:
        load.start()
    barrier = pltpu.get_barrier_semaphore()

    @pl.loop(1, PIECES)
    def _(k):
        pl.semaphore_signal(barrier, inc=1, device_id={"seq": (me + k) % PIECES}, device_id_type=MESH)

    for peer in (far, above, below):
        pl.semaphore_signal(barrier, inc=1, device_id={"chan": peer}, device_id_type=MESH)

    gathered[pl.ds(blocks * GROUPS, 16), :] = jnp.zeros((16, length), BF16)
    gated[pl.ds(blocks, 16), :] = jnp.zeros((16, 2 * length), BF16)
    position = (me * length + lax.broadcasted_iota(jnp.int32, (16, length), 1)).astype(F32)
    for load in loads[:4]:
        load.wait()
    row = beside(rate_in[...], jnp.zeros((1, 2 * SIDE - blocks), F32))
    rate[...] = jnp.broadcast_to(row, (SIDE, 2 * SIDE)).T

    @pl.loop(0, pairs)
    def _(p):
        r = pl.ds(pl.multiple_of(16 * p, 16), 16)
        sig = key[r, :].astype(F32) * value[r, :].astype(F32)
        speed = rate[r, :1]
        window = jnp.sqrt(1.0 - jnp.exp(-2.0 * speed)) * jnp.exp(-speed * position)
        envelope[r, :] = window
        ker = filt[r, :] * window
        send1[2 * p] = stacked(sig[:8], ker[:8]).astype(BF16)
        send1[2 * p + 1] = stacked(sig[8:], ker[8:]).astype(BF16)

    loads[4].wait()
    pl.semaphore_wait(barrier, PIECES - 1 + 3)

    def gather_copy(index, slot, chunk, target):
        begin, count = CHUNKS[chunk]
        rows = gathered.at[pl.ds(pl.multiple_of(blocks * slot + begin, 16), count)]
        return pltpu.make_async_remote_copy(
            src_ref=rows,
            dst_ref=rows,
            send_sem=ag_send.at[index, chunk],
            recv_sem=ag_recv.at[slot, chunk],
            device_id={"chan": target},
            device_id_type=MESH,
        )

    span = range(len(CHUNKS))
    middle = len(CHUNKS) // 2
    above_far = above + 1 - 2 * (above % 2)
    below_far = below + 1 - 2 * (below % 2)

    def relay(index, from_below, from_above, chunk):
        if chunk < middle:
            return gather_copy(index, from_below, chunk, above)
        return gather_copy(index, from_above, chunk, below)

    def to_owners(source, landing, send_sem, recv_sem):
        @pl.loop(1, PIECES)
        def _(k):
            target = (me + k) % PIECES

            @pl.when(target < owners)
            def _():
                go(exchange(me, target, source, landing, send_sem, recv_sem))

        @pl.when(owner)
        def _():
            landing[me] = source[me]

    def pass_far(c):
        land(gather_copy(0, far, c, far))
        go(gather_copy(3, far, c, above))
        go(gather_copy(4, far, c, below))

    for c in span[:FLIGHT]:
        go(gather_copy(0, group, c, far))
    for c in span:
        go(gather_copy(1, group, c, above))
        go(gather_copy(2, group, (c + middle) % len(CHUNKS), below))
    for load in loads[5:]:
        load.wait()
    first[...] = first_in[...].astype(BF16)
    for i, part in enumerate((0, 1, 0)):
        rows = pl.ds(2 * SIDE * i, 2 * SIDE)
        forward[rows, :] = forward_in[part].astype(BF16)
        backward[rows, :] = backward_in[part].astype(BF16)
        last[:, rows] = last_in[part].astype(BF16)
    if A1POS == 0:
        to_owners(send1, recv1, ss1, rs1)
    for c in span:
        pass_far(c)
        if c + FLIGHT < len(CHUNKS):
            go(gather_copy(0, group, c + FLIGHT, far))
        if c + 1 == A1POS:
            to_owners(send1, recv1, ss1, rs1)
        if c + 1 == OWNPOS:
            for d in span:
                land(relay(5, below, above, d))
                go(relay(5, below, above, d))
    for c in span:
        land(relay(6, below_far, above_far, c))
        go(relay(6, below_far, above_far, c))

    @pl.when(owner)
    def _():
        @pl.loop(0, PIECES)
        def _(s):
            @pl.when(s != me)
            def _():
                land(arrival(s, send1, recv1, ss1, rs1))

        @pl.loop(0, PIECES, unroll=4)
        def _(s):
            piece = recv1[s].astype(F32)
            for i in range(4):
                rows1[pl.ds(pl.multiple_of((s * 4 + i) * 16, 16), 16), :] = piece[:, i * SIDE : (i + 1) * SIDE]

        @pl.loop(0, OWNED // BATCH)
        def _(b):
            cs = [b * BATCH + i for i in range(BATCH)]
            sig = [rows1[pl.ds(c, SIDE, stride=16), :].astype(BF16) for c in cs]
            ker = [rows1[pl.ds(c + 8, SIDE, stride=16), :].astype(BF16) for c in cs]
            spec = forward_pair(jnp.concatenate(sig + ker, 1), first, twist, forward, 2 * BATCH)
            specs[b] = spec
            y = backward_pair(
                product(spec[: SIDE * BATCH], spec[SIDE * BATCH :]), twist, backward, last, BATCH
            )
            for i, c in enumerate(cs):
                out1[pl.ds(c, SIDE, stride=8), :] = y[:, i * SIDE : (i + 1) * SIDE]

        @pl.loop(0, PIECES, unroll=4)
        def _(s):
            t = [out1[pl.ds(pl.multiple_of((s * 4 + i) * 8, 8), 8), :] for i in range(4)]
            send3[s] = beside(stacked(t[0], t[2]), stacked(t[1], t[3])).astype(BF16)

        @pl.loop(1, PIECES)
        def _(k):
            go(exchange(me, (me + k) % PIECES, send3, recv3, ss3, rs3))

        recv3[me] = send3[me]

    for c in span:
        if c < middle:
            land(gather_copy(0, above, c, above))
            land(gather_copy(0, above_far, c, above))
        else:
            land(gather_copy(0, below, c, below))
            land(gather_copy(0, below_far, c, below))
        opposite = (group + 4) % GROUPS
        land(gather_copy(0, opposite, c, above))
        land(gather_copy(0, opposite + 1 - 2 * (opposite % 2), c, above))
    depth = blocks * GROUPS
    for n in range(length // HALF):
        cols = pl.ds(n * HALF, HALF)
        upstream[:, cols] = dot(weight[...], gathered[pl.ds(0, depth), cols])

    @pl.loop(0, pairs)
    def _(p):
        r = pl.ds(pl.multiple_of(16 * p, 16), 16)
        g = upstream[r, :] * gate[r, :].astype(F32)
        send2[2 * p] = stacked(g[:8, :HALF], g[:8, HALF:]).astype(BF16)
        send2[2 * p + 1] = stacked(g[8:, :HALF], g[8:, HALF:]).astype(BF16)

    to_owners(send2, recv2, ss2, rs2)

    def from_owners(source, landing, send_sem, recv_sem):
        @pl.loop(0, owners)
        def _(s):
            @pl.when(s != me)
            def _():
                land(arrival(s, source, landing, send_sem, recv_sem))

    from_owners(send3, recv3, ss3, rs3)

    @pl.loop(0, pairs)
    def _(p):
        r = pl.ds(pl.multiple_of(16 * p, 16), 16)
        a = recv3[2 * p].astype(F32)
        b = recv3[2 * p + 1].astype(F32)
        conv = stacked(beside(a[:8], a[8:]), beside(b[:8], b[8:]))
        gate_grad[r, :] = (upstream[r, :] * conv).astype(BF16)
        high, low = split(gate[r, :].astype(F32) * conv)
        gated[r, :] = beside(high, low)

    for j in range(GROUPS):
        rows = gathered[pl.ds(blocks * j, HALF), :]
        term = lax.dot_general(
            beside(rows, rows), gated[...], (((1,), (1,)), ((), ())), preferred_element_type=F32
        )
        for g in range(4):
            partial[g % 2, 2 * j + g // 2] = term[60 * g : 60 * g + 64]

    core_copy = pltpu.make_async_remote_copy(
        src_ref=partial.at[1 - core],
        dst_ref=core_in,
        send_sem=core_send,
        recv_sem=core_recv,
        device_id={"seq": sibling},
        device_id_type=MESH,
    )
    go(core_copy)

    def x_copy(k):
        there = (x + k) % 4
        return pltpu.make_async_remote_copy(
            src_ref=chip_sum.at[pl.ds(4 * there, 4)],
            dst_ref=x_in.at[k - 1],
            send_sem=x_send.at[k - 1],
            recv_sem=x_recv.at[k - 1],
            device_id={"seq": (me + 8 * k) % PIECES},
            device_id_type=MESH,
        )

    land(core_copy)
    partial[core] = partial[core] + core_in[...]
    chip_sum[...] = partial[core].astype(BF16)
    for k in (1, 2, 3):
        go(x_copy(k))

    @pl.when(owner)
    def _():
        @pl.loop(0, PIECES)
        def _(s):
            @pl.when(s != me)
            def _():
                land(arrival(s, send2, recv2, ss2, rs2))

        @pl.loop(0, PIECES, unroll=4)
        def _(s):
            piece = recv2[s].astype(F32)
            for i in range(4):
                h, l = i // 2, i % 2
                rows2[pl.ds(pl.multiple_of((s * 4 + i) * 8, 8), 8), :] = piece[
                    h * 8 : h * 8 + 8, l * SIDE : (l + 1) * SIDE
                ]

    def correlate(b):
        @pl.when(owner)
        def _():
            cs = [b * BATCH + i for i in range(BATCH)]
            g = [rows2[pl.ds(c, SIDE, stride=8), :].astype(BF16) for c in cs]
            gspec = forward_pair(jnp.concatenate(g, 1), first, twist, forward, BATCH)
            spec = specs[b]
            both = stacked(
                product_conj(spec[SIDE * BATCH :], gspec), product_conj(spec[: SIDE * BATCH], gspec)
            )
            y = backward_pair(both, twist, backward, last, 2 * BATCH)
            for i in range(2 * BATCH):
                out2[pl.ds(i, SIDE, stride=8), :] = y[:, i * SIDE : (i + 1) * SIDE]

            @pl.loop(0, PIECES, unroll=4)
            def _(s):
                t = [out2[pl.ds(pl.multiple_of((s * 4 + i) * 8, 8), 8), :] for i in range(4)]
                send4[b, s] = beside(stacked(t[0], t[2]), stacked(t[1], t[3])).astype(BF16)

            @pl.loop(1, PIECES)
            def _(k):
                go(exchange(me, (me + k) % PIECES, send4.at[b], recv4.at[b], ss4.at[b], rs4.at[b]))

            recv4[b, me] = send4[b, me]

    correlate(0)

    correlate(1)

    for k in (1, 2, 3):
        land(x_copy(k))
    x_sum[...] = partial[core, pl.ds(4 * x, 4)] + x_in[0].astype(F32) + x_in[1].astype(F32) + x_in[2].astype(F32)

    def z_copy(k):
        there = (z + k) % 4
        return pltpu.make_async_remote_copy(
            src_ref=x_out.at[there],
            dst_ref=z_in.at[k - 1],
            send_sem=z_send.at[k - 1],
            recv_sem=z_recv.at[k - 1],
            device_id={"seq": x * 8 + there * 2 + core},
            device_id_type=MESH,
        )

    x_out[...] = x_sum[...].astype(BF16)
    for k in (1, 2, 3):
        go(z_copy(k))

    for b in range(2):
        from_owners(send4.at[b], recv4.at[b], ss4.at[b], rs4.at[b])

    @pl.loop(0, pairs)
    def _(p):
        r = pl.ds(pl.multiple_of(16 * p, 16), 16)
        parts = []
        for o in range(2):
            for b in range(2):
                a = recv4[b, 2 * p + o].astype(F32)
                parts.append(beside(a[:8], a[8:]))
        sgrad = jnp.concatenate([a[:4] for a in parts], 0)
        kgrad = jnp.concatenate([a[4:] for a in parts], 0)
        key_grad[r, :] = (sgrad * value[r, :].astype(F32)).astype(BF16)
        value_grad[r, :] = (sgrad * key[r, :].astype(F32)).astype(BF16)
        filter_grad[r, :] = kgrad * envelope[r, :]

    for k in (1, 2, 3):
        land(z_copy(k))
    total = x_sum[z] + z_in[0].astype(F32) + z_in[1].astype(F32) + z_in[2].astype(F32)
    weight_grad[...] = total[: weight_grad.shape[0], :blocks]

    for k in (1, 2, 3):
        leave(x_copy(k))
        leave(z_copy(k))
    leave(core_copy)
    for c in span:
        leave(gather_copy(0, group, c, far))
        leave(gather_copy(1, group, c, above))
        leave(gather_copy(2, group, c, below))
        leave(gather_copy(3, far, c, above))
        leave(gather_copy(4, far, c, below))
        leave(relay(5, below, above, c))
        leave(relay(6, below_far, above_far, c))

    @pl.loop(1, PIECES)
    def _(k):
        target = (me + k) % PIECES

        @pl.when(target < owners)
        def _():
            leave(exchange(me, target, send1, recv1, ss1, rs1))
            leave(exchange(me, target, send2, recv2, ss2, rs2))

        @pl.when(owner)
        def _():
            leave(exchange(me, target, send3, recv3, ss3, rs3))
            for b in range(2):
                leave(exchange(me, target, send4.at[b], recv4.at[b], ss4.at[b], rs4.at[b]))


def settle_kernel(*refs):
    count = len(refs) // 3
    arrivals, departures = refs[-2], refs[-1]
    inward = [pltpu.make_async_copy(refs[i], refs[2 * count + i], arrivals.at[i]) for i in range(count)]
    outward = [pltpu.make_async_copy(refs[2 * count + i], refs[count + i], departures.at[i]) for i in range(count)]
    for copy in inward:
        copy.start()
    for copy, onward in zip(inward, outward):
        copy.wait()
        onward.start()
    for onward in outward:
        onward.wait()


def per_device(gate_act, key_act, value_act, filter_raw, decay_rate, out_weight, out_grad):
    channels, length = gate_act.shape
    tables = [jnp.asarray(t) for t in make_tables()]
    shape = (channels, length)
    vmem = pltpu.VMEM
    dma = pltpu.SemaphoreType.DMA
    rows = SIDE * OWNED
    results = pl.pallas_call(
        whole_kernel,
        out_shape=(
            jax.ShapeDtypeStruct(shape, BF16),
            jax.ShapeDtypeStruct(shape, BF16),
            jax.ShapeDtypeStruct(shape, BF16),
            jax.ShapeDtypeStruct(shape, F32),
            jax.ShapeDtypeStruct((channels * GROUPS // PIECES, channels), F32),
        ),
        in_specs=[pl.BlockSpec(memory_space=pltpu.HBM)] * 12,
        scratch_shapes=[
            vmem(shape, BF16),
            vmem(shape, BF16),
            vmem(shape, BF16),
            vmem(shape, F32),
            vmem((1, channels), F32),
            vmem((2 * SIDE, SIDE), F32),
            vmem(out_weight.shape, BF16),
        ]
        + [vmem(t.shape, t.dtype) for t in tables]
        + [
            vmem((2 * SIDE, 2 * SIDE), BF16),
            vmem((6 * SIDE, 2 * SIDE), BF16),
            vmem((6 * SIDE, 2 * SIDE), BF16),
            vmem((SIDE, 6 * SIDE), BF16),
            vmem((PIECES, 16, length), BF16),
            vmem((PIECES, 16, length), BF16),
            vmem((PIECES, 16, HALF), BF16),
            vmem((PIECES, 16, HALF), BF16),
            vmem((PIECES, 16, HALF), BF16),
            vmem((PIECES, 16, HALF), BF16),
            vmem((2, PIECES, 16, HALF), BF16),
            vmem((2, PIECES, 16, HALF), BF16),
            vmem((channels * GROUPS + 16, length), BF16),
            vmem(shape, F32),
            vmem(shape, F32),
            vmem((2 * rows, SIDE), F32),
            vmem((rows, SIDE), F32),
            vmem((OWNED // BATCH, 2 * SIDE * BATCH, 2 * SIDE), F32),
            vmem((rows, SIDE), F32),
            vmem((rows, SIDE), F32),
            vmem((channels + 16, 2 * length), BF16),
            vmem((2, 16, 64, HALF), F32),
            vmem((16, 64, HALF), F32),
            vmem((16, 64, HALF), BF16),
            vmem((3, 4, 64, HALF), BF16),
            vmem((4, 64, HALF), F32),
            vmem((4, 64, HALF), BF16),
            vmem((3, 64, HALF), BF16),
            dma((12,)),
        ]
        + [dma((PIECES,))] * 6
        + [dma((2, PIECES))] * 2
        + [dma((7, len(CHUNKS))), dma((GROUPS, len(CHUNKS))), dma, dma]
        + [dma((3,))] * 4,
        compiler_params=pltpu.CompilerParams(
            collective_id=0, has_side_effects=True, vmem_limit_bytes=LIMIT
        ),
    )(gate_act, key_act, value_act, filter_raw, decay_rate[None, :], out_weight, out_grad, *tables)
    *grads, weight_grad = pl.pallas_call(
        settle_kernel,
        out_shape=tuple(jax.ShapeDtypeStruct(r.shape, r.dtype) for r in results),
        in_specs=[pl.BlockSpec(memory_space=pltpu.HBM)] * 5,
        out_specs=[pl.BlockSpec(memory_space=pltpu.HBM)] * 5,
        scratch_shapes=[vmem(r.shape, r.dtype) for r in results] + [dma((5,))] * 2,
        compiler_params=pltpu.CompilerParams(vmem_limit_bytes=LIMIT),
    )(*results)
    return (*grads, weight_grad.T)


def solution(mesh):
    rows = P("chan", "seq")
    return jax.shard_map(
        per_device,
        mesh=mesh,
        in_specs=(rows, rows, rows, rows, P("chan"), P("chan", None), rows),
        out_specs=(rows,) * 5,
        check_vma=False,
    )
```

```python
import functools
import math

import jax
import jax.numpy as jnp
import numpy as np
from jax import lax
from jax.experimental import pallas as pl
from jax.experimental.pallas import tpu as pltpu
from jax.sharding import PartitionSpec as P

F32 = jnp.float32
BF16 = jnp.bfloat16
SIDE = 128
LENGTH = SIDE * SIDE
OWNED = 8
PIECES = 32
GROUPS = 8
HALF = 256
BATCH = 4
THIRDS = 3
LIMIT = 63 * 2**20
CHUNKS = ((0, 48), (48, 32), (80, 48), (128, 32), (160, 48), (208, 32))
FLIGHT = 3
A1POS = 0
OWNPOS = 2
MESH = pl.DeviceIdType.MESH


def halves(table):
    high = np.asarray(table, np.float32).astype(jnp.bfloat16)
    low = (np.asarray(table, np.float64) - high.astype(np.float64)).astype(np.float32).astype(jnp.bfloat16)
    return high, low


def make_tables():
    n = np.arange(SIDE, dtype=np.float64)
    outer = 2.0 * np.pi * np.outer(n + 0.25, n) / SIDE
    first = np.concatenate([np.cos(outer), -np.sin(outer)], 0)
    first_high, first_low = halves(first)
    first_both = np.concatenate([first_high, first_low], 1)
    turn = 2.0 * np.pi * np.outer(n + 0.25, n) / LENGTH
    twist = np.stack([np.cos(turn), np.sin(turn)]).astype(np.float32)
    inner = 2.0 * np.pi * np.outer(n, n) / SIDE
    cosine, sine = np.cos(inner), np.sin(inner)
    forward = np.concatenate([np.concatenate([cosine, -sine], 1), np.concatenate([sine, cosine], 1)], 0)
    backward = np.concatenate([np.concatenate([cosine, sine], 1), np.concatenate([-sine, cosine], 1)], 0)
    last = np.concatenate([np.cos(outer.T), -np.sin(outer.T)], 1) / LENGTH
    return (
        first_both.astype(np.float32),
        twist,
        np.stack(halves(forward)).astype(np.float32),
        np.stack(halves(backward)).astype(np.float32),
        np.stack(halves(last)).astype(np.float32),
    )


def dot(a, b):
    return jnp.dot(a, b, preferred_element_type=F32)


def split(x):
    high = x.astype(BF16)
    return high, (x - high.astype(F32)).astype(BF16)


def forward_pair(x, first, twist, forward, count):
    a = dot(first[...], jnp.concatenate([x, x], 0))
    cosine, sine = twist[0], twist[1]
    rows = []
    for i in range(count):
        real = a[:SIDE, i * SIDE : (i + 1) * SIDE]
        imag = a[SIDE:, i * SIDE : (i + 1) * SIDE]
        rows.append(jnp.concatenate([real * cosine + imag * sine, imag * cosine - real * sine], 1))
    high, low = split(jnp.concatenate(rows, 0))
    return dot(jnp.concatenate([high, high, low], 1), forward[...])


def backward_pair(spec, twist, backward, last, count):
    high, low = split(spec)
    d = dot(jnp.concatenate([high, high, low], 1), backward[...])
    cosine, sine = twist[0], twist[1]
    columns = []
    for i in range(count):
        real = d[i * SIDE : (i + 1) * SIDE, :SIDE]
        imag = d[i * SIDE : (i + 1) * SIDE, SIDE:]
        columns.append(jnp.concatenate([real * cosine - imag * sine, imag * cosine + real * sine], 0))
    high, low = split(jnp.concatenate(columns, 1))
    return dot(last[...], jnp.concatenate([high, high, low], 0))


def product(a, b):
    ar, ai, br, bi = a[:, :SIDE], a[:, SIDE:], b[:, :SIDE], b[:, SIDE:]
    return jnp.concatenate([ar * br - ai * bi, ar * bi + ai * br], 1)


def product_conj(a, b):
    ar, ai, br, bi = a[:, :SIDE], a[:, SIDE:], b[:, :SIDE], b[:, SIDE:]
    return jnp.concatenate([ar * br + ai * bi, ar * bi - ai * br], 1)


def go(copy):
    copy.start()


def land(copy):
    copy.wait_recv()


def leave(copy):
    copy.wait_send()


def exchange(me, target, source, landing, send_sem, recv_sem):
    return pltpu.make_async_remote_copy(
        src_ref=source.at[target],
        dst_ref=landing.at[me],
        send_sem=send_sem,
        recv_sem=recv_sem,
        device_id={"seq": target},
        device_id_type=MESH,
    )


def all_of(count, peer, source, landing, send_sem, recv_sem):
    return pltpu.make_async_remote_copy(
        src_ref=source.at[pl.ds(0, count)],
        dst_ref=landing.at[pl.ds(0, count)],
        send_sem=send_sem,
        recv_sem=recv_sem,
        device_id={"seq": peer},
        device_id_type=MESH,
    )


def third(source, target, sem, index, part):
    total = source.shape[0]
    count = total // THIRDS // 8 * 8
    begin = part * count
    rows = pl.ds(begin, count if part < THIRDS - 1 else total - begin)
    return pltpu.make_async_copy(source.at[rows], target.at[rows], sem.at[index, part])


def stacked(upper, lower):
    return jnp.concatenate([upper, lower], 0)


def beside(left, right):
    return jnp.concatenate([left, right], 1)


def whole_kernel(
    gate_hbm, key_hbm, value_hbm, filt_hbm, rate_hbm, weight_hbm, cotangent_hbm,
    first_hbm, twist_hbm, forward_hbm, backward_hbm, last_hbm,
    gate_grad_hbm, key_grad_hbm, value_grad_hbm, filter_grad_hbm, weight_grad_hbm,
    gate_grad, key_grad, value_grad, filter_grad, weight_grad, out_sem,
    gate, key, value, filt, rate_in, rate, weight, first_in, twist, forward_in, backward_in, last_in,
    first, forward, backward, last,
    send1, recv1, send2, recv2, send3, recv3, send4, recv4,
    gathered, upstream, envelope, rows1, rows2, specs, out1, out2, gated,
    partial, core_in, chip_sum, x_in, x_sum, x_out, z_in, in_sem,
    ss1, rs1, ss2, rs2, ss3, rs3, ss4, rs4, ag_send, ag_recv, core_send, core_recv, x_send, x_recv, z_send, z_recv,
):
    me = lax.axis_index("seq")
    group = lax.axis_index("chan")
    blocks = gate.shape[0]
    length = gate.shape[1]
    owners = blocks // OWNED
    core = me % 2
    sibling = me + 1 - 2 * core
    z = (me // 2) % 4
    x = me // 8
    far = group + 1 - 2 * (group % 2)
    above = (group + 2) % GROUPS
    below = (group + GROUPS - 2) % GROUPS
    pairs = owners // 2
    owner = me < owners
    own_rows = pl.ds(pl.multiple_of(blocks * group, 16), blocks)

    loads = [
        pltpu.make_async_copy(a, b, in_sem.at[i])
        for i, (a, b) in enumerate(
            (
                (key_hbm, key),
                (value_hbm, value),
                (filt_hbm, filt),
                (rate_hbm, rate_in),
                (cotangent_hbm, gathered.at[own_rows]),
                (gate_hbm, gate),
                (first_hbm, first_in),
                (twist_hbm, twist),
                (forward_hbm, forward_in),
                (backward_hbm, backward_in),
                (last_hbm, last_in),
                (weight_hbm, weight),
            )
        )
    ]
    for load in loads:
        load.start()
    barrier = pltpu.get_barrier_semaphore()

    @pl.loop(1, PIECES)
    def _(k):
        pl.semaphore_signal(barrier, inc=1, device_id={"seq": (me + k) % PIECES}, device_id_type=MESH)

    for peer in (far, above, below):
        pl.semaphore_signal(barrier, inc=1, device_id={"chan": peer}, device_id_type=MESH)

    gathered[pl.ds(blocks * GROUPS, 16), :] = jnp.zeros((16, length), BF16)
    gated[pl.ds(blocks, 16), :] = jnp.zeros((16, 2 * length), BF16)
    position = (me * length + lax.broadcasted_iota(jnp.int32, (16, length), 1)).astype(F32)
    for load in loads[:4]:
        load.wait()
    row = beside(rate_in[...], jnp.zeros((1, 2 * SIDE - blocks), F32))
    rate[...] = jnp.broadcast_to(row, (SIDE, 2 * SIDE)).T

    @pl.loop(0, pairs)
    def _(p):
        r = pl.ds(pl.multiple_of(16 * p, 16), 16)
        sig = key[r, :].astype(F32) * value[r, :].astype(F32)
        speed = rate[r, :1]
        window = jnp.sqrt(1.0 - jnp.exp(-2.0 * speed)) * jnp.exp(-speed * position)
        envelope[r, :] = window
        ker = filt[r, :] * window
        send1[2 * p] = stacked(sig[:8], ker[:8]).astype(BF16)
        send1[2 * p + 1] = stacked(sig[8:], ker[8:]).astype(BF16)

    loads[4].wait()
    pl.semaphore_wait(barrier, PIECES - 1 + 3)

    def gather_copy(slot, chunk, target):
        begin, count = CHUNKS[chunk]
        rows = gathered.at[pl.ds(pl.multiple_of(blocks * slot + begin, 16), count)]
        return pltpu.make_async_remote_copy(
            src_ref=rows,
            dst_ref=rows,
            send_sem=ag_send,
            recv_sem=ag_recv.at[slot, chunk],
            device_id={"chan": target},
            device_id_type=MESH,
        )

    span = range(len(CHUNKS))
    middle = len(CHUNKS) // 2
    above_far = above + 1 - 2 * (above % 2)
    below_far = below + 1 - 2 * (below % 2)

    def relay(from_below, from_above, chunk):
        if chunk < middle:
            return gather_copy(from_below, chunk, above)
        return gather_copy(from_above, chunk, below)

    def to_owners(source, landing, send_sem, recv_sem):
        @pl.loop(1, PIECES)
        def _(k):
            target = (me + k) % PIECES

            @pl.when(target < owners)
            def _():
                go(exchange(me, target, source, landing, send_sem, recv_sem))

        @pl.when(owner)
        def _():
            landing[me] = source[me]

    def pass_far(c):
        land(gather_copy(far, c, far))
        go(gather_copy(far, c, above))
        go(gather_copy(far, c, below))

    for c in span[:FLIGHT]:
        go(gather_copy(group, c, far))
    for c in span:
        go(gather_copy(group, c, above))
        go(gather_copy(group, (c + middle) % len(CHUNKS), below))
    for load in loads[5:]:
        load.wait()
    first[...] = first_in[...].astype(BF16)
    for i, part in enumerate((0, 1, 0)):
        rows = pl.ds(2 * SIDE * i, 2 * SIDE)
        forward[rows, :] = forward_in[part].astype(BF16)
        backward[rows, :] = backward_in[part].astype(BF16)
        last[:, rows] = last_in[part].astype(BF16)
    if A1POS == 0:
        to_owners(send1, recv1, ss1, rs1)
    for c in span:
        pass_far(c)
        if c + FLIGHT < len(CHUNKS):
            go(gather_copy(group, c + FLIGHT, far))
        if c + 1 == A1POS:
            to_owners(send1, recv1, ss1, rs1)
        if c + 1 == OWNPOS:
            for d in span:
                land(relay(below, above, d))
                go(relay(below, above, d))
    for c in span:
        land(relay(below_far, above_far, c))
        go(relay(below_far, above_far, c))

    @pl.when(owner)
    def _():
        land(all_of(PIECES - 1, sibling, send1, recv1, ss1, rs1))

        @pl.loop(0, PIECES, unroll=4)
        def _(s):
            piece = recv1[s].astype(F32)
            for i in range(4):
                rows1[pl.ds(pl.multiple_of((s * 4 + i) * 16, 16), 16), :] = piece[:, i * SIDE : (i + 1) * SIDE]

        @pl.loop(0, OWNED // BATCH)
        def _(b):
            cs = [b * BATCH + i for i in range(BATCH)]
            sig = [rows1[pl.ds(c, SIDE, stride=16), :].astype(BF16) for c in cs]
            ker = [rows1[pl.ds(c + 8, SIDE, stride=16), :].astype(BF16) for c in cs]
            spec = forward_pair(jnp.concatenate(sig + ker, 1), first, twist, forward, 2 * BATCH)
            specs[b] = spec
            y = backward_pair(
                product(spec[: SIDE * BATCH], spec[SIDE * BATCH :]), twist, backward, last, BATCH
            )
            for i, c in enumerate(cs):
                out1[pl.ds(c, SIDE, stride=8), :] = y[:, i * SIDE : (i + 1) * SIDE]

        @pl.loop(0, PIECES, unroll=4)
        def _(s):
            t = [out1[pl.ds(pl.multiple_of((s * 4 + i) * 8, 8), 8), :] for i in range(4)]
            send3[s] = beside(stacked(t[0], t[2]), stacked(t[1], t[3])).astype(BF16)

        @pl.loop(1, PIECES)
        def _(k):
            go(exchange(me, (me + k) % PIECES, send3, recv3, ss3, rs3))

        recv3[me] = send3[me]

    for c in span:
        if c < middle:
            land(gather_copy(above, c, above))
            land(gather_copy(above_far, c, above))
        else:
            land(gather_copy(below, c, below))
            land(gather_copy(below_far, c, below))
        opposite = (group + 4) % GROUPS
        land(gather_copy(opposite, c, above))
        land(gather_copy(opposite + 1 - 2 * (opposite % 2), c, above))
    depth = blocks * GROUPS
    for n in range(length // HALF):
        cols = pl.ds(n * HALF, HALF)
        upstream[:, cols] = dot(weight[...], gathered[pl.ds(0, depth), cols])

    @pl.loop(0, pairs)
    def _(p):
        r = pl.ds(pl.multiple_of(16 * p, 16), 16)
        g = upstream[r, :] * gate[r, :].astype(F32)
        send2[2 * p] = stacked(g[:8, :HALF], g[:8, HALF:]).astype(BF16)
        send2[2 * p + 1] = stacked(g[8:, :HALF], g[8:, HALF:]).astype(BF16)

    to_owners(send2, recv2, ss2, rs2)

    def from_owners(source, landing, send_sem, recv_sem):
        @pl.when(owner)
        def _():
            land(all_of(owners - 1, sibling, source, landing, send_sem, recv_sem))

        @pl.when(me >= owners)
        def _():
            land(all_of(owners, sibling, source, landing, send_sem, recv_sem))

    from_owners(send3, recv3, ss3, rs3)

    @pl.loop(0, pairs)
    def _(p):
        r = pl.ds(pl.multiple_of(16 * p, 16), 16)
        a = recv3[2 * p].astype(F32)
        b = recv3[2 * p + 1].astype(F32)
        conv = stacked(beside(a[:8], a[8:]), beside(b[:8], b[8:]))
        gate_grad[r, :] = (upstream[r, :] * conv).astype(BF16)
        high, low = split(gate[r, :].astype(F32) * conv)
        gated[r, :] = beside(high, low)

    for t in range(THIRDS):
        third(gate_grad, gate_grad_hbm, out_sem, 0, t).start()

    for j in range(GROUPS):
        rows = gathered[pl.ds(blocks * j, HALF), :]
        term = lax.dot_general(
            beside(rows, rows), gated[...], (((1,), (1,)), ((), ())), preferred_element_type=F32
        )
        for g in range(4):
            partial[g % 2, 2 * j + g // 2] = term[60 * g : 60 * g + 64]

    core_copy = pltpu.make_async_remote_copy(
        src_ref=partial.at[1 - core],
        dst_ref=core_in,
        send_sem=core_send,
        recv_sem=core_recv,
        device_id={"seq": sibling},
        device_id_type=MESH,
    )
    go(core_copy)

    def x_copy(k):
        there = (x + k) % 4
        return pltpu.make_async_remote_copy(
            src_ref=chip_sum.at[pl.ds(4 * there, 4)],
            dst_ref=x_in.at[k - 1],
            send_sem=x_send.at[k - 1],
            recv_sem=x_recv.at[k - 1],
            device_id={"seq": (me + 8 * k) % PIECES},
            device_id_type=MESH,
        )

    land(core_copy)
    partial[core] = partial[core] + core_in[...]
    chip_sum[...] = partial[core].astype(BF16)
    for k in (1, 2, 3):
        go(x_copy(k))

    @pl.when(owner)
    def _():
        land(all_of(PIECES - 1, sibling, send2, recv2, ss2, rs2))

        @pl.loop(0, PIECES, unroll=4)
        def _(s):
            piece = recv2[s].astype(F32)
            for i in range(4):
                h, l = i // 2, i % 2
                rows2[pl.ds(pl.multiple_of((s * 4 + i) * 8, 8), 8), :] = piece[
                    h * 8 : h * 8 + 8, l * SIDE : (l + 1) * SIDE
                ]

    def correlate(b):
        @pl.when(owner)
        def _():
            cs = [b * BATCH + i for i in range(BATCH)]
            g = [rows2[pl.ds(c, SIDE, stride=8), :].astype(BF16) for c in cs]
            gspec = forward_pair(jnp.concatenate(g, 1), first, twist, forward, BATCH)
            spec = specs[b]
            both = stacked(
                product_conj(spec[SIDE * BATCH :], gspec), product_conj(spec[: SIDE * BATCH], gspec)
            )
            y = backward_pair(both, twist, backward, last, 2 * BATCH)
            for i in range(2 * BATCH):
                out2[pl.ds(i, SIDE, stride=8), :] = y[:, i * SIDE : (i + 1) * SIDE]

            @pl.loop(0, PIECES, unroll=4)
            def _(s):
                t = [out2[pl.ds(pl.multiple_of((s * 4 + i) * 8, 8), 8), :] for i in range(4)]
                send4[b, s] = beside(stacked(t[0], t[2]), stacked(t[1], t[3])).astype(BF16)

            @pl.loop(1, PIECES)
            def _(k):
                go(exchange(me, (me + k) % PIECES, send4.at[b], recv4.at[b], ss4.at[b], rs4.at[b]))

            recv4[b, me] = send4[b, me]

    correlate(0)

    correlate(1)

    for k in (1, 2, 3):
        land(x_copy(k))
    x_sum[...] = partial[core, pl.ds(4 * x, 4)] + x_in[0].astype(F32) + x_in[1].astype(F32) + x_in[2].astype(F32)

    def z_copy(k):
        there = (z + k) % 4
        return pltpu.make_async_remote_copy(
            src_ref=x_out.at[there],
            dst_ref=z_in.at[k - 1],
            send_sem=z_send.at[k - 1],
            recv_sem=z_recv.at[k - 1],
            device_id={"seq": x * 8 + there * 2 + core},
            device_id_type=MESH,
        )

    x_out[...] = x_sum[...].astype(BF16)
    for k in (1, 2, 3):
        go(z_copy(k))

    for b in range(2):
        from_owners(send4.at[b], recv4.at[b], ss4.at[b], rs4.at[b])

    outs = ((key_grad, key_grad_hbm), (value_grad, value_grad_hbm), (filter_grad, filter_grad_hbm))
    for t in range(THIRDS):
        @pl.loop(t * pairs // THIRDS, (t + 1) * pairs // THIRDS)
        def _(p):
            r = pl.ds(pl.multiple_of(16 * p, 16), 16)
            parts = []
            for o in range(2):
                for b in range(2):
                    a = recv4[b, 2 * p + o].astype(F32)
                    parts.append(beside(a[:8], a[8:]))
            sgrad = jnp.concatenate([a[:4] for a in parts], 0)
            kgrad = jnp.concatenate([a[4:] for a in parts], 0)
            key_grad[r, :] = (sgrad * value[r, :].astype(F32)).astype(BF16)
            value_grad[r, :] = (sgrad * key[r, :].astype(F32)).astype(BF16)
            filter_grad[r, :] = kgrad * envelope[r, :]

        for n, (source, target) in enumerate(outs):
            third(source, target, out_sem, 1 + n, t).start()

    for k in (1, 2, 3):
        land(z_copy(k))
    total = x_sum[z] + z_in[0].astype(F32) + z_in[1].astype(F32) + z_in[2].astype(F32)
    weight_grad[...] = total[: weight_grad.shape[0], :blocks]
    weight_out = pltpu.make_async_copy(weight_grad, weight_grad_hbm, out_sem.at[4, 0])
    weight_out.start()

    for k in (1, 2, 3):
        leave(x_copy(k))
        leave(z_copy(k))
    leave(core_copy)
    sent = gathered.at[pl.ds(0, 7 * blocks)]
    leave(
        pltpu.make_async_remote_copy(
            src_ref=sent,
            dst_ref=sent,
            send_sem=ag_send,
            recv_sem=ag_recv.at[0, 0],
            device_id={"chan": far},
            device_id_type=MESH,
        )
    )

    @pl.when(owner)
    def _():
        leave(all_of(owners - 1, sibling, send1, recv1, ss1, rs1))
        leave(all_of(owners - 1, sibling, send2, recv2, ss2, rs2))
        leave(all_of(PIECES - 1, sibling, send3, recv3, ss3, rs3))
        for b in range(2):
            leave(all_of(PIECES - 1, sibling, send4.at[b], recv4.at[b], ss4.at[b], rs4.at[b]))

    @pl.when(me >= owners)
    def _():
        leave(all_of(owners, sibling, send1, recv1, ss1, rs1))
        leave(all_of(owners, sibling, send2, recv2, ss2, rs2))

    for t in range(THIRDS):
        third(gate_grad, gate_grad_hbm, out_sem, 0, t).wait()
        for n, (source, target) in enumerate(outs):
            third(source, target, out_sem, 1 + n, t).wait()
    weight_out.wait()


def settle_kernel(*refs):
    count = len(refs) // 3
    inward, outward = [], []
    for i in range(count):
        for t in range(THIRDS):
            inward.append(third(refs[i], refs[2 * count + i], refs[-2], i, t))
            outward.append(third(refs[2 * count + i], refs[count + i], refs[-1], i, t))
    for copy in inward:
        copy.start()
    for copy, onward in zip(inward, outward):
        copy.wait()
        onward.start()
    for onward in outward:
        onward.wait()


def per_device(gate_act, key_act, value_act, filter_raw, decay_rate, out_weight, out_grad):
    channels, length = gate_act.shape
    tables = [jnp.asarray(t) for t in make_tables()]
    shape = (channels, length)
    vmem = pltpu.VMEM
    dma = pltpu.SemaphoreType.DMA
    rows = SIDE * OWNED
    results = pl.pallas_call(
        whole_kernel,
        out_shape=(
            jax.ShapeDtypeStruct(shape, BF16),
            jax.ShapeDtypeStruct(shape, BF16),
            jax.ShapeDtypeStruct(shape, BF16),
            jax.ShapeDtypeStruct(shape, F32),
            jax.ShapeDtypeStruct((channels * GROUPS // PIECES, channels), F32),
        ),
        in_specs=[pl.BlockSpec(memory_space=pltpu.HBM)] * 12,
        out_specs=(pl.BlockSpec(memory_space=pltpu.HBM),) * 5,
        scratch_shapes=[
            vmem(shape, BF16),
            vmem(shape, BF16),
            vmem(shape, BF16),
            vmem(shape, F32),
            vmem((channels * GROUPS // PIECES, channels), F32),
            dma((5, THIRDS)),
            vmem(shape, BF16),
            vmem(shape, BF16),
            vmem(shape, BF16),
            vmem(shape, F32),
            vmem((1, channels), F32),
            vmem((2 * SIDE, SIDE), F32),
            vmem(out_weight.shape, BF16),
        ]
        + [vmem(t.shape, t.dtype) for t in tables]
        + [
            vmem((2 * SIDE, 2 * SIDE), BF16),
            vmem((6 * SIDE, 2 * SIDE), BF16),
            vmem((6 * SIDE, 2 * SIDE), BF16),
            vmem((SIDE, 6 * SIDE), BF16),
            vmem((PIECES, 16, length), BF16),
            vmem((PIECES, 16, length), BF16),
            vmem((PIECES, 16, HALF), BF16),
            vmem((PIECES, 16, HALF), BF16),
            vmem((PIECES, 16, HALF), BF16),
            vmem((PIECES, 16, HALF), BF16),
            vmem((2, PIECES, 16, HALF), BF16),
            vmem((2, PIECES, 16, HALF), BF16),
            vmem((channels * GROUPS + 16, length), BF16),
            vmem(shape, F32),
            vmem(shape, F32),
            vmem((2 * rows, SIDE), F32),
            vmem((rows, SIDE), F32),
            vmem((OWNED // BATCH, 2 * SIDE * BATCH, 2 * SIDE), F32),
            vmem((rows, SIDE), F32),
            vmem((rows, SIDE), F32),
            vmem((channels + 16, 2 * length), BF16),
            vmem((2, 16, 64, HALF), F32),
            vmem((16, 64, HALF), F32),
            vmem((16, 64, HALF), BF16),
            vmem((3, 4, 64, HALF), BF16),
            vmem((4, 64, HALF), F32),
            vmem((4, 64, HALF), BF16),
            vmem((3, 64, HALF), BF16),
            dma((12,)),
        ]
        + [dma] * 6
        + [dma((2,))] * 2
        + [dma, dma((GROUPS, len(CHUNKS))), dma, dma]
        + [dma((3,))] * 4,
        compiler_params=pltpu.CompilerParams(
            collective_id=0, has_side_effects=True, vmem_limit_bytes=LIMIT
        ),
    )(gate_act, key_act, value_act, filter_raw, decay_rate[None, :], out_weight, out_grad, *tables)
    *grads, weight_grad = pl.pallas_call(
        settle_kernel,
        out_shape=tuple(jax.ShapeDtypeStruct(r.shape, r.dtype) for r in results),
        in_specs=[pl.BlockSpec(memory_space=pltpu.HBM)] * 5,
        out_specs=[pl.BlockSpec(memory_space=pltpu.HBM)] * 5,
        scratch_shapes=[vmem(r.shape, r.dtype) for r in results] + [dma((5, THIRDS))] * 2,
        compiler_params=pltpu.CompilerParams(vmem_limit_bytes=LIMIT),
    )(*results)
    return (*grads, weight_grad.T)


def solution(mesh):
    rows = P("chan", "seq")
    return jax.shard_map(
        per_device,
        mesh=mesh,
        in_specs=(rows, rows, rows, rows, P("chan"), P("chan", None), rows),
        out_specs=(rows,) * 5,
        check_vma=False,
    )
```

```python
import functools
import math

import jax
import jax.numpy as jnp
import numpy as np
from jax import lax
from jax.experimental import pallas as pl
from jax.experimental.pallas import tpu as pltpu
from jax.sharding import PartitionSpec as P

F32 = jnp.float32
BF16 = jnp.bfloat16
SIDE = 128
LENGTH = SIDE * SIDE
OWNED = 8
PIECES = 32
GROUPS = 8
HALF = 256
BATCH = 4
THIRDS = 3
LIMIT = 63 * 2**20
CHUNKS = ((0, 48), (48, 32), (80, 48), (128, 32), (160, 48), (208, 32))
FLIGHT = 3
A1POS = 2
OWNPOS = 2
MESH = pl.DeviceIdType.MESH


def halves(table):
    high = np.asarray(table, np.float32).astype(jnp.bfloat16)
    low = (np.asarray(table, np.float64) - high.astype(np.float64)).astype(np.float32).astype(jnp.bfloat16)
    return high, low


def make_tables():
    n = np.arange(SIDE, dtype=np.float64)
    outer = 2.0 * np.pi * np.outer(n + 0.25, n) / SIDE
    first = np.concatenate([np.cos(outer), -np.sin(outer)], 0)
    first_high, first_low = halves(first)
    first_both = np.concatenate([first_high, first_low], 1)
    turn = 2.0 * np.pi * np.outer(n + 0.25, n) / LENGTH
    twist = np.stack([np.cos(turn), np.sin(turn)]).astype(np.float32)
    inner = 2.0 * np.pi * np.outer(n, n) / SIDE
    cosine, sine = np.cos(inner), np.sin(inner)
    forward = np.concatenate([np.concatenate([cosine, -sine], 1), np.concatenate([sine, cosine], 1)], 0)
    backward = np.concatenate([np.concatenate([cosine, sine], 1), np.concatenate([-sine, cosine], 1)], 0)
    last = np.concatenate([np.cos(outer.T), -np.sin(outer.T)], 1) / LENGTH
    return (
        first_both.astype(np.float32),
        twist,
        np.stack(halves(forward)).astype(np.float32),
        np.stack(halves(backward)).astype(np.float32),
        np.stack(halves(last)).astype(np.float32),
    )


def dot(a, b):
    return jnp.dot(a, b, preferred_element_type=F32)


def split(x):
    high = x.astype(BF16)
    return high, (x - high.astype(F32)).astype(BF16)


def forward_pair(x, first, twist, forward, count):
    a = dot(first[...], jnp.concatenate([x, x], 0))
    cosine, sine = twist[0], twist[1]
    rows = []
    for i in range(count):
        real = a[:SIDE, i * SIDE : (i + 1) * SIDE]
        imag = a[SIDE:, i * SIDE : (i + 1) * SIDE]
        rows.append(jnp.concatenate([real * cosine + imag * sine, imag * cosine - real * sine], 1))
    high, low = split(jnp.concatenate(rows, 0))
    return dot(jnp.concatenate([high, high, low], 1), forward[...])


def backward_pair(spec, twist, backward, last, count):
    high, low = split(spec)
    d = dot(jnp.concatenate([high, high, low], 1), backward[...])
    cosine, sine = twist[0], twist[1]
    columns = []
    for i in range(count):
        real = d[i * SIDE : (i + 1) * SIDE, :SIDE]
        imag = d[i * SIDE : (i + 1) * SIDE, SIDE:]
        columns.append(jnp.concatenate([real * cosine - imag * sine, imag * cosine + real * sine], 0))
    high, low = split(jnp.concatenate(columns, 1))
    return dot(last[...], jnp.concatenate([high, high, low], 0))


def product(a, b):
    ar, ai, br, bi = a[:, :SIDE], a[:, SIDE:], b[:, :SIDE], b[:, SIDE:]
    return jnp.concatenate([ar * br - ai * bi, ar * bi + ai * br], 1)


def product_conj(a, b):
    ar, ai, br, bi = a[:, :SIDE], a[:, SIDE:], b[:, :SIDE], b[:, SIDE:]
    return jnp.concatenate([ar * br + ai * bi, ar * bi - ai * br], 1)


def go(copy):
    copy.start()


def land(copy):
    copy.wait_recv()


def leave(copy):
    copy.wait_send()


def exchange(me, target, source, landing, send_sem, recv_sem):
    return pltpu.make_async_remote_copy(
        src_ref=source.at[target],
        dst_ref=landing.at[me],
        send_sem=send_sem,
        recv_sem=recv_sem,
        device_id={"seq": target},
        device_id_type=MESH,
    )


def all_of(count, peer, source, landing, send_sem, recv_sem):
    return pltpu.make_async_remote_copy(
        src_ref=source.at[pl.ds(0, count)],
        dst_ref=landing.at[pl.ds(0, count)],
        send_sem=send_sem,
        recv_sem=recv_sem,
        device_id={"seq": peer},
        device_id_type=MESH,
    )


def third(source, target, sem, index, part):
    total = source.shape[0]
    count = total // THIRDS // 8 * 8
    begin = part * count
    rows = pl.ds(begin, count if part < THIRDS - 1 else total - begin)
    return pltpu.make_async_copy(source.at[rows], target.at[rows], sem.at[index, part])


def stacked(upper, lower):
    return jnp.concatenate([upper, lower], 0)


def beside(left, right):
    return jnp.concatenate([left, right], 1)


def whole_kernel(
    gate_hbm, key_hbm, value_hbm, filt_hbm, rate_hbm, weight_hbm, cotangent_hbm,
    first_hbm, twist_hbm, forward_hbm, backward_hbm, last_hbm,
    gate_grad_hbm, key_grad_hbm, value_grad_hbm, filter_grad_hbm, weight_grad_hbm,
    gate_grad, key_grad, value_grad, filter_grad, weight_grad, out_sem,
    gate, key, value, filt, rate_in, rate, weight, first_in, twist, forward_in, backward_in, last_in,
    first, forward, backward, last,
    send1, recv1, send2, recv2, send3, recv3, send4, recv4,
    gathered, upstream, envelope, rows1, rows2, specs, out1, out2, gated,
    partial, core_in, chip_sum, x_in, x_sum, x_out, z_in, in_sem,
    ss1, rs1, ss2, rs2, ss3, rs3, ss4, rs4, ag_send, ag_recv, core_send, core_recv, x_send, x_recv, z_send, z_recv,
):
    me = lax.axis_index("seq")
    group = lax.axis_index("chan")
    blocks = gate.shape[0]
    length = gate.shape[1]
    owners = blocks // OWNED
    core = me % 2
    sibling = me + 1 - 2 * core
    z = (me // 2) % 4
    x = me // 8
    far = group + 1 - 2 * (group % 2)
    above = (group + 2) % GROUPS
    below = (group + GROUPS - 2) % GROUPS
    pairs = owners // 2
    owner = me < owners
    own_rows = pl.ds(pl.multiple_of(blocks * group, 16), blocks)

    loads = [
        pltpu.make_async_copy(a, b, in_sem.at[i])
        for i, (a, b) in enumerate(
            (
                (key_hbm, key),
                (value_hbm, value),
                (filt_hbm, filt),
                (rate_hbm, rate_in),
                (cotangent_hbm, gathered.at[own_rows]),
                (gate_hbm, gate),
                (first_hbm, first_in),
                (twist_hbm, twist),
                (forward_hbm, forward_in),
                (backward_hbm, backward_in),
                (last_hbm, last_in),
                (weight_hbm, weight),
            )
        )
    ]
    for load in loads:
        load.start()
    barrier = pltpu.get_barrier_semaphore()

    @pl.loop(1, PIECES)
    def _(k):
        pl.semaphore_signal(barrier, inc=1, device_id={"seq": (me + k) % PIECES}, device_id_type=MESH)

    for peer in (far, above, below):
        pl.semaphore_signal(barrier, inc=1, device_id={"chan": peer}, device_id_type=MESH)

    gathered[pl.ds(blocks * GROUPS, 16), :] = jnp.zeros((16, length), BF16)
    gated[pl.ds(blocks, 16), :] = jnp.zeros((16, 2 * length), BF16)
    position = (me * length + lax.broadcasted_iota(jnp.int32, (16, length), 1)).astype(F32)
    for load in loads[:4]:
        load.wait()
    row = beside(rate_in[...], jnp.zeros((1, 2 * SIDE - blocks), F32))
    rate[...] = jnp.broadcast_to(row, (SIDE, 2 * SIDE)).T

    @pl.loop(0, pairs)
    def _(p):
        r = pl.ds(pl.multiple_of(16 * p, 16), 16)
        sig = key[r, :].astype(F32) * value[r, :].astype(F32)
        speed = rate[r, :1]
        window = jnp.sqrt(1.0 - jnp.exp(-2.0 * speed)) * jnp.exp(-speed * position)
        envelope[r, :] = window
        ker = filt[r, :] * window
        send1[2 * p] = stacked(sig[:8], ker[:8]).astype(BF16)
        send1[2 * p + 1] = stacked(sig[8:], ker[8:]).astype(BF16)

    loads[4].wait()
    pl.semaphore_wait(barrier, PIECES - 1 + 3)

    def gather_copy(slot, chunk, target):
        begin, count = CHUNKS[chunk]
        rows = gathered.at[pl.ds(pl.multiple_of(blocks * slot + begin, 16), count)]
        return pltpu.make_async_remote_copy(
            src_ref=rows,
            dst_ref=rows,
            send_sem=ag_send,
            recv_sem=ag_recv.at[slot, chunk],
            device_id={"chan": target},
            device_id_type=MESH,
        )

    span = range(len(CHUNKS))
    middle = len(CHUNKS) // 2
    above_far = above + 1 - 2 * (above % 2)
    below_far = below + 1 - 2 * (below % 2)

    def relay(from_below, from_above, chunk):
        if chunk < middle:
            return gather_copy(from_below, chunk, above)
        return gather_copy(from_above, chunk, below)

    def to_owners(source, landing, send_sem, recv_sem):
        @pl.loop(1, PIECES)
        def _(k):
            target = (me + k) % PIECES

            @pl.when(target < owners)
            def _():
                go(exchange(me, target, source, landing, send_sem, recv_sem))

        @pl.when(owner)
        def _():
            landing[me] = source[me]

    def pass_far(c):
        land(gather_copy(far, c, far))
        go(gather_copy(far, c, above))
        go(gather_copy(far, c, below))

    for c in span[:FLIGHT]:
        go(gather_copy(group, c, far))
    for c in span:
        go(gather_copy(group, c, above))
        go(gather_copy(group, (c + middle) % len(CHUNKS), below))
    for load in loads[5:]:
        load.wait()
    first[...] = first_in[...].astype(BF16)
    for i, part in enumerate((0, 1, 0)):
        rows = pl.ds(2 * SIDE * i, 2 * SIDE)
        forward[rows, :] = forward_in[part].astype(BF16)
        backward[rows, :] = backward_in[part].astype(BF16)
        last[:, rows] = last_in[part].astype(BF16)
    if A1POS == 0:
        to_owners(send1, recv1, ss1, rs1)
    for c in span:
        pass_far(c)
        if c + FLIGHT < len(CHUNKS):
            go(gather_copy(group, c + FLIGHT, far))
        if c + 1 == A1POS:
            to_owners(send1, recv1, ss1, rs1)
        if c + 1 == OWNPOS:
            for d in span:
                land(relay(below, above, d))
                go(relay(below, above, d))
    for c in span:
        land(relay(below_far, above_far, c))
        go(relay(below_far, above_far, c))

    @pl.when(owner)
    def _():
        land(all_of(PIECES - 1, sibling, send1, recv1, ss1, rs1))

        @pl.loop(0, PIECES, unroll=4)
        def _(s):
            piece = recv1[s].astype(F32)
            for i in range(4):
                rows1[pl.ds(pl.multiple_of((s * 4 + i) * 16, 16), 16), :] = piece[:, i * SIDE : (i + 1) * SIDE]

        @pl.loop(0, OWNED // BATCH)
        def _(b):
            cs = [b * BATCH + i for i in range(BATCH)]
            sig = [rows1[pl.ds(c, SIDE, stride=16), :].astype(BF16) for c in cs]
            ker = [rows1[pl.ds(c + 8, SIDE, stride=16), :].astype(BF16) for c in cs]
            spec = forward_pair(jnp.concatenate(sig + ker, 1), first, twist, forward, 2 * BATCH)
            specs[b] = spec
            y = backward_pair(
                product(spec[: SIDE * BATCH], spec[SIDE * BATCH :]), twist, backward, last, BATCH
            )
            for i in range(BATCH):
                out1[pl.ds(i, SIDE, stride=BATCH), :] = y[:, i * SIDE : (i + 1) * SIDE]

            @pl.loop(0, PIECES, unroll=4)
            def _(s):
                send3[b, s] = out1[pl.ds(pl.multiple_of(s * 16, 16), 16), :].astype(BF16)

            @pl.loop(1, PIECES)
            def _(k):
                go(exchange(me, (me + k) % PIECES, send3.at[b], recv3.at[b], ss3.at[b], rs3.at[b]))

            recv3[b, me] = send3[b, me]

    for c in span:
        if c < middle:
            land(gather_copy(above, c, above))
            land(gather_copy(above_far, c, above))
        else:
            land(gather_copy(below, c, below))
            land(gather_copy(below_far, c, below))
        opposite = (group + 4) % GROUPS
        land(gather_copy(opposite, c, above))
        land(gather_copy(opposite + 1 - 2 * (opposite % 2), c, above))
    depth = blocks * GROUPS
    for n in range(length // HALF):
        cols = pl.ds(n * HALF, HALF)
        upstream[:, cols] = dot(weight[...], gathered[pl.ds(0, depth), cols])

    @pl.loop(0, pairs)
    def _(p):
        r = pl.ds(pl.multiple_of(16 * p, 16), 16)
        g = upstream[r, :] * gate[r, :].astype(F32)
        for o in range(2):
            for b in range(2):
                q = g[8 * o + 4 * b : 8 * o + 4 * b + 4]
                quarters = [q[:, i * SIDE : (i + 1) * SIDE] for i in range(4)]
                send2[b, 2 * p + o] = jnp.concatenate(quarters, 0).astype(BF16)

    for b in range(2):
        to_owners(send2.at[b], recv2.at[b], ss2.at[b], rs2.at[b])

    def from_owners(source, landing, send_sem, recv_sem):
        @pl.when(owner)
        def _():
            land(all_of(owners - 1, sibling, source, landing, send_sem, recv_sem))

        @pl.when(me >= owners)
        def _():
            land(all_of(owners, sibling, source, landing, send_sem, recv_sem))

    for b in range(2):
        from_owners(send3.at[b], recv3.at[b], ss3.at[b], rs3.at[b])

    @pl.loop(0, pairs)
    def _(p):
        r = pl.ds(pl.multiple_of(16 * p, 16), 16)
        parts = []
        for o in range(2):
            for b in range(2):
                a = recv3[b, 2 * p + o].astype(F32)
                parts.append(jnp.concatenate([a[4 * i : 4 * i + 4] for i in range(4)], 1))
        conv = jnp.concatenate(parts, 0)
        gate_grad[r, :] = (upstream[r, :] * conv).astype(BF16)
        high, low = split(gate[r, :].astype(F32) * conv)
        gated[r, :] = beside(high, low)

    for t in range(THIRDS):
        third(gate_grad, gate_grad_hbm, out_sem, 0, t).start()

    for j in range(GROUPS):
        rows = gathered[pl.ds(blocks * j, HALF), :]
        term = lax.dot_general(
            beside(rows, rows), gated[...], (((1,), (1,)), ((), ())), preferred_element_type=F32
        )
        for g in range(4):
            partial[g % 2, 2 * j + g // 2] = term[60 * g : 60 * g + 64]

    core_copy = pltpu.make_async_remote_copy(
        src_ref=partial.at[1 - core],
        dst_ref=core_in,
        send_sem=core_send,
        recv_sem=core_recv,
        device_id={"seq": sibling},
        device_id_type=MESH,
    )
    go(core_copy)

    def x_copy(k):
        there = (x + k) % 4
        return pltpu.make_async_remote_copy(
            src_ref=chip_sum.at[pl.ds(4 * there, 4)],
            dst_ref=x_in.at[k - 1],
            send_sem=x_send.at[k - 1],
            recv_sem=x_recv.at[k - 1],
            device_id={"seq": (me + 8 * k) % PIECES},
            device_id_type=MESH,
        )

    land(core_copy)
    partial[core] = partial[core] + core_in[...]
    chip_sum[...] = partial[core].astype(BF16)
    for k in (1, 2, 3):
        go(x_copy(k))

    def correlate(b):
        @pl.when(owner)
        def _():
            land(all_of(PIECES - 1, sibling, send2.at[b], recv2.at[b], ss2.at[b], rs2.at[b]))

            @pl.loop(0, PIECES, unroll=4)
            def _(s):
                rows2[pl.ds(pl.multiple_of(s * 16, 16), 16), :] = recv2[b, s].astype(F32)

            g = [rows2[pl.ds(i, SIDE, stride=BATCH), :].astype(BF16) for i in range(BATCH)]
            gspec = forward_pair(jnp.concatenate(g, 1), first, twist, forward, BATCH)
            spec = specs[b]
            both = stacked(
                product_conj(spec[SIDE * BATCH :], gspec), product_conj(spec[: SIDE * BATCH], gspec)
            )
            y = backward_pair(both, twist, backward, last, 2 * BATCH)
            for i in range(2 * BATCH):
                out2[pl.ds(i, SIDE, stride=8), :] = y[:, i * SIDE : (i + 1) * SIDE]

            @pl.loop(0, PIECES, unroll=4)
            def _(s):
                t = [out2[pl.ds(pl.multiple_of((s * 4 + i) * 8, 8), 8), :] for i in range(4)]
                send4[b, s] = beside(stacked(t[0], t[2]), stacked(t[1], t[3])).astype(BF16)

            @pl.loop(1, PIECES)
            def _(k):
                go(exchange(me, (me + k) % PIECES, send4.at[b], recv4.at[b], ss4.at[b], rs4.at[b]))

            recv4[b, me] = send4[b, me]

    correlate(0)

    correlate(1)

    for k in (1, 2, 3):
        land(x_copy(k))
    x_sum[...] = partial[core, pl.ds(4 * x, 4)] + x_in[0].astype(F32) + x_in[1].astype(F32) + x_in[2].astype(F32)

    def z_copy(k):
        there = (z + k) % 4
        return pltpu.make_async_remote_copy(
            src_ref=x_out.at[there],
            dst_ref=z_in.at[k - 1],
            send_sem=z_send.at[k - 1],
            recv_sem=z_recv.at[k - 1],
            device_id={"seq": x * 8 + there * 2 + core},
            device_id_type=MESH,
        )

    x_out[...] = x_sum[...].astype(BF16)
    for k in (1, 2, 3):
        go(z_copy(k))

    for b in range(2):
        from_owners(send4.at[b], recv4.at[b], ss4.at[b], rs4.at[b])

    outs = ((key_grad, key_grad_hbm), (value_grad, value_grad_hbm), (filter_grad, filter_grad_hbm))
    for t in range(THIRDS):
        @pl.loop(t * pairs // THIRDS, (t + 1) * pairs // THIRDS)
        def _(p):
            r = pl.ds(pl.multiple_of(16 * p, 16), 16)
            parts = []
            for o in range(2):
                for b in range(2):
                    a = recv4[b, 2 * p + o].astype(F32)
                    parts.append(beside(a[:8], a[8:]))
            sgrad = jnp.concatenate([a[:4] for a in parts], 0)
            kgrad = jnp.concatenate([a[4:] for a in parts], 0)
            key_grad[r, :] = (sgrad * value[r, :].astype(F32)).astype(BF16)
            value_grad[r, :] = (sgrad * key[r, :].astype(F32)).astype(BF16)
            filter_grad[r, :] = kgrad * envelope[r, :]

        for n, (source, target) in enumerate(outs):
            third(source, target, out_sem, 1 + n, t).start()

    for k in (1, 2, 3):
        land(z_copy(k))
    total = x_sum[z] + z_in[0].astype(F32) + z_in[1].astype(F32) + z_in[2].astype(F32)
    weight_grad[...] = total[: weight_grad.shape[0], :blocks]
    weight_out = pltpu.make_async_copy(weight_grad, weight_grad_hbm, out_sem.at[4, 0])
    weight_out.start()

    for k in (1, 2, 3):
        leave(x_copy(k))
        leave(z_copy(k))
    leave(core_copy)
    sent = gathered.at[pl.ds(0, 7 * blocks)]
    leave(
        pltpu.make_async_remote_copy(
            src_ref=sent,
            dst_ref=sent,
            send_sem=ag_send,
            recv_sem=ag_recv.at[0, 0],
            device_id={"chan": far},
            device_id_type=MESH,
        )
    )

    @pl.when(owner)
    def _():
        leave(all_of(owners - 1, sibling, send1, recv1, ss1, rs1))
        for b in range(2):
            leave(all_of(owners - 1, sibling, send2.at[b], recv2.at[b], ss2.at[b], rs2.at[b]))
            leave(all_of(PIECES - 1, sibling, send3.at[b], recv3.at[b], ss3.at[b], rs3.at[b]))
            leave(all_of(PIECES - 1, sibling, send4.at[b], recv4.at[b], ss4.at[b], rs4.at[b]))

    @pl.when(me >= owners)
    def _():
        leave(all_of(owners, sibling, send1, recv1, ss1, rs1))
        for b in range(2):
            leave(all_of(owners, sibling, send2.at[b], recv2.at[b], ss2.at[b], rs2.at[b]))

    for t in range(THIRDS):
        third(gate_grad, gate_grad_hbm, out_sem, 0, t).wait()
        for n, (source, target) in enumerate(outs):
            third(source, target, out_sem, 1 + n, t).wait()
    weight_out.wait()


def settle_kernel(*refs):
    count = len(refs) // 3
    inward, outward = [], []
    for i in range(count):
        for t in range(THIRDS):
            inward.append(third(refs[i], refs[2 * count + i], refs[-2], i, t))
            outward.append(third(refs[2 * count + i], refs[count + i], refs[-1], i, t))
    for copy in inward:
        copy.start()
    for copy, onward in zip(inward, outward):
        copy.wait()
        onward.start()
    for onward in outward:
        onward.wait()


def per_device(gate_act, key_act, value_act, filter_raw, decay_rate, out_weight, out_grad):
    channels, length = gate_act.shape
    tables = [jnp.asarray(t) for t in make_tables()]
    shape = (channels, length)
    vmem = pltpu.VMEM
    dma = pltpu.SemaphoreType.DMA
    rows = SIDE * OWNED
    results = pl.pallas_call(
        whole_kernel,
        out_shape=(
            jax.ShapeDtypeStruct(shape, BF16),
            jax.ShapeDtypeStruct(shape, BF16),
            jax.ShapeDtypeStruct(shape, BF16),
            jax.ShapeDtypeStruct(shape, F32),
            jax.ShapeDtypeStruct((channels * GROUPS // PIECES, channels), F32),
        ),
        in_specs=[pl.BlockSpec(memory_space=pltpu.HBM)] * 12,
        out_specs=(pl.BlockSpec(memory_space=pltpu.HBM),) * 5,
        scratch_shapes=[
            vmem(shape, BF16),
            vmem(shape, BF16),
            vmem(shape, BF16),
            vmem(shape, F32),
            vmem((channels * GROUPS // PIECES, channels), F32),
            dma((5, THIRDS)),
            vmem(shape, BF16),
            vmem(shape, BF16),
            vmem(shape, BF16),
            vmem(shape, F32),
            vmem((1, channels), F32),
            vmem((2 * SIDE, SIDE), F32),
            vmem(out_weight.shape, BF16),
        ]
        + [vmem(t.shape, t.dtype) for t in tables]
        + [
            vmem((2 * SIDE, 2 * SIDE), BF16),
            vmem((6 * SIDE, 2 * SIDE), BF16),
            vmem((6 * SIDE, 2 * SIDE), BF16),
            vmem((SIDE, 6 * SIDE), BF16),
            vmem((PIECES, 16, length), BF16),
            vmem((PIECES, 16, length), BF16),
            vmem((2, PIECES, 16, SIDE), BF16),
            vmem((2, PIECES, 16, SIDE), BF16),
            vmem((2, PIECES, 16, SIDE), BF16),
            vmem((2, PIECES, 16, SIDE), BF16),
            vmem((2, PIECES, 16, HALF), BF16),
            vmem((2, PIECES, 16, HALF), BF16),
            vmem((channels * GROUPS + 16, length), BF16),
            vmem(shape, F32),
            vmem(shape, F32),
            vmem((2 * rows, SIDE), F32),
            vmem((SIDE * BATCH, SIDE), F32),
            vmem((OWNED // BATCH, 2 * SIDE * BATCH, 2 * SIDE), F32),
            vmem((SIDE * BATCH, SIDE), F32),
            vmem((rows, SIDE), F32),
            vmem((channels + 16, 2 * length), BF16),
            vmem((2, 16, 64, HALF), F32),
            vmem((16, 64, HALF), F32),
            vmem((16, 64, HALF), BF16),
            vmem((3, 4, 64, HALF), BF16),
            vmem((4, 64, HALF), F32),
            vmem((4, 64, HALF), BF16),
            vmem((3, 64, HALF), BF16),
            dma((12,)),
        ]
        + [dma] * 2
        + [dma((2,))] * 6
        + [dma, dma((GROUPS, len(CHUNKS))), dma, dma]
        + [dma((3,))] * 4,
        compiler_params=pltpu.CompilerParams(
            collective_id=0, has_side_effects=True, vmem_limit_bytes=LIMIT
        ),
    )(gate_act, key_act, value_act, filter_raw, decay_rate[None, :], out_weight, out_grad, *tables)
    *grads, weight_grad = pl.pallas_call(
        settle_kernel,
        out_shape=tuple(jax.ShapeDtypeStruct(r.shape, r.dtype) for r in results),
        in_specs=[pl.BlockSpec(memory_space=pltpu.HBM)] * 5,
        out_specs=[pl.BlockSpec(memory_space=pltpu.HBM)] * 5,
        scratch_shapes=[vmem(r.shape, r.dtype) for r in results] + [dma((5, THIRDS))] * 2,
        compiler_params=pltpu.CompilerParams(vmem_limit_bytes=LIMIT),
    )(*results)
    return (*grads, weight_grad.T)


def solution(mesh):
    rows = P("chan", "seq")
    return jax.shard_map(
        per_device,
        mesh=mesh,
        in_specs=(rows, rows, rows, rows, P("chan"), P("chan", None), rows),
        out_specs=(rows,) * 5,
        check_vma=False,
    )
```

```python
import functools
import math

import jax
import jax.numpy as jnp
import numpy as np
from jax import lax
from jax.experimental import pallas as pl
from jax.experimental.pallas import tpu as pltpu
from jax.sharding import PartitionSpec as P

F32 = jnp.float32
BF16 = jnp.bfloat16
SIDE = 128
LENGTH = SIDE * SIDE
OWNED = 8
PIECES = 32
GROUPS = 8
HALF = 256
BATCH = 4
THIRDS = 3
LIMIT = 63 * 2**20
CHUNKS = ((0, 48), (48, 32), (80, 48), (128, 32), (160, 48), (208, 32))
FLIGHT = 3
A1POS = 2
OWNPOS = 1
MESH = pl.DeviceIdType.MESH


def halves(table):
    high = np.asarray(table, np.float32).astype(jnp.bfloat16)
    low = (np.asarray(table, np.float64) - high.astype(np.float64)).astype(np.float32).astype(jnp.bfloat16)
    return high, low


def make_tables():
    n = np.arange(SIDE, dtype=np.float64)
    outer = 2.0 * np.pi * np.outer(n + 0.25, n) / SIDE
    first = np.concatenate([np.cos(outer), -np.sin(outer)], 0)
    first_high, first_low = halves(first)
    first_both = np.concatenate([first_high, first_low], 1)
    turn = 2.0 * np.pi * np.outer(n + 0.25, n) / LENGTH
    twist = np.stack([np.cos(turn), np.sin(turn)]).astype(np.float32)
    inner = 2.0 * np.pi * np.outer(n, n) / SIDE
    cosine, sine = np.cos(inner), np.sin(inner)
    forward = np.concatenate([np.concatenate([cosine, -sine], 1), np.concatenate([sine, cosine], 1)], 0)
    backward = np.concatenate([np.concatenate([cosine, sine], 1), np.concatenate([-sine, cosine], 1)], 0)
    last = np.concatenate([np.cos(outer.T), -np.sin(outer.T)], 1) / LENGTH
    return (
        first_both.astype(np.float32),
        twist,
        np.stack(halves(forward)).astype(np.float32),
        np.stack(halves(backward)).astype(np.float32),
        np.stack(halves(last)).astype(np.float32),
    )


def dot(a, b):
    return jnp.dot(a, b, preferred_element_type=F32)


def split(x):
    high = x.astype(BF16)
    return high, (x - high.astype(F32)).astype(BF16)


def forward_pair(x, first, twist, forward, count):
    a = dot(first[...], jnp.concatenate([x, x], 0))
    cosine, sine = twist[0], twist[1]
    rows = []
    for i in range(count):
        real = a[:SIDE, i * SIDE : (i + 1) * SIDE]
        imag = a[SIDE:, i * SIDE : (i + 1) * SIDE]
        rows.append(jnp.concatenate([real * cosine + imag * sine, imag * cosine - real * sine], 1))
    high, low = split(jnp.concatenate(rows, 0))
    return dot(jnp.concatenate([high, high, low], 1), forward[...])


def backward_pair(spec, twist, backward, last, count):
    high, low = split(spec)
    d = dot(jnp.concatenate([high, high, low], 1), backward[...])
    cosine, sine = twist[0], twist[1]
    columns = []
    for i in range(count):
        real = d[i * SIDE : (i + 1) * SIDE, :SIDE]
        imag = d[i * SIDE : (i + 1) * SIDE, SIDE:]
        columns.append(jnp.concatenate([real * cosine - imag * sine, imag * cosine + real * sine], 0))
    high, low = split(jnp.concatenate(columns, 1))
    return dot(last[...], jnp.concatenate([high, high, low], 0))


def product(a, b):
    ar, ai, br, bi = a[:, :SIDE], a[:, SIDE:], b[:, :SIDE], b[:, SIDE:]
    return jnp.concatenate([ar * br - ai * bi, ar * bi + ai * br], 1)


def product_conj(a, b):
    ar, ai, br, bi = a[:, :SIDE], a[:, SIDE:], b[:, :SIDE], b[:, SIDE:]
    return jnp.concatenate([ar * br + ai * bi, ar * bi - ai * br], 1)


def go(copy):
    copy.start()


def land(copy):
    copy.wait_recv()


def leave(copy):
    copy.wait_send()


def exchange(me, target, source, landing, send_sem, recv_sem):
    return pltpu.make_async_remote_copy(
        src_ref=source.at[target],
        dst_ref=landing.at[me],
        send_sem=send_sem,
        recv_sem=recv_sem,
        device_id={"seq": target},
        device_id_type=MESH,
    )


def all_of(count, peer, source, landing, send_sem, recv_sem):
    return pltpu.make_async_remote_copy(
        src_ref=source.at[pl.ds(0, count)],
        dst_ref=landing.at[pl.ds(0, count)],
        send_sem=send_sem,
        recv_sem=recv_sem,
        device_id={"seq": peer},
        device_id_type=MESH,
    )


def third(source, target, sem, index, part):
    total = source.shape[0]
    count = total // THIRDS // 8 * 8
    begin = part * count
    rows = pl.ds(begin, count if part < THIRDS - 1 else total - begin)
    return pltpu.make_async_copy(source.at[rows], target.at[rows], sem.at[index, part])


def stacked(upper, lower):
    return jnp.concatenate([upper, lower], 0)


def beside(left, right):
    return jnp.concatenate([left, right], 1)


def whole_kernel(
    gate_hbm, key_hbm, value_hbm, filt_hbm, rate_hbm, weight_hbm, cotangent_hbm,
    first_hbm, twist_hbm, forward_hbm, backward_hbm, last_hbm,
    gate_grad_hbm, key_grad_hbm, value_grad_hbm, filter_grad_hbm, weight_grad_hbm,
    gate_grad, key_grad, value_grad, filter_grad, weight_grad, out_sem,
    gate, key, value, filt, rate_in, rate, weight, first_in, twist, forward_in, backward_in, last_in,
    first, forward, backward, last,
    send1, recv1, send2, recv2, send3, recv3, send4, recv4,
    gathered, upstream, envelope, rows1, rows2, specs, out1, out2, gated,
    partial, core_in, chip_sum, x_in, x_sum, x_out, z_in, in_sem,
    ss1, rs1, ss2, rs2, ss3, rs3, ss4, rs4, ag_send, ag_recv, core_send, core_recv, x_send, x_recv, z_send, z_recv,
):
    me = lax.axis_index("seq")
    group = lax.axis_index("chan")
    blocks = gate.shape[0]
    length = gate.shape[1]
    owners = blocks // OWNED
    core = me % 2
    sibling = me + 1 - 2 * core
    z = (me // 2) % 4
    x = me // 8
    far = group + 1 - 2 * (group % 2)
    above = (group + 2) % GROUPS
    below = (group + GROUPS - 2) % GROUPS
    pairs = owners // 2
    owner = me < owners
    own_rows = pl.ds(pl.multiple_of(blocks * group, 16), blocks)

    loads = [
        pltpu.make_async_copy(a, b, in_sem.at[i])
        for i, (a, b) in enumerate(
            (
                (key_hbm, key),
                (value_hbm, value),
                (filt_hbm, filt),
                (rate_hbm, rate_in),
                (cotangent_hbm, gathered.at[own_rows]),
                (gate_hbm, gate),
                (first_hbm, first_in),
                (twist_hbm, twist),
                (forward_hbm, forward_in),
                (backward_hbm, backward_in),
                (last_hbm, last_in),
                (weight_hbm, weight),
            )
        )
    ]
    for load in loads:
        load.start()
    barrier = pltpu.get_barrier_semaphore()

    @pl.loop(1, PIECES)
    def _(k):
        pl.semaphore_signal(barrier, inc=1, device_id={"seq": (me + k) % PIECES}, device_id_type=MESH)

    for peer in (far, above, below):
        pl.semaphore_signal(barrier, inc=1, device_id={"chan": peer}, device_id_type=MESH)

    gathered[pl.ds(blocks * GROUPS, 16), :] = jnp.zeros((16, length), BF16)
    gated[pl.ds(blocks, 16), :] = jnp.zeros((16, 2 * length), BF16)
    position = (me * length + lax.broadcasted_iota(jnp.int32, (16, length), 1)).astype(F32)
    for load in loads[:4]:
        load.wait()
    row = beside(rate_in[...], jnp.zeros((1, 2 * SIDE - blocks), F32))
    rate[...] = jnp.broadcast_to(row, (SIDE, 2 * SIDE)).T

    @pl.loop(0, pairs)
    def _(p):
        r = pl.ds(pl.multiple_of(16 * p, 16), 16)
        sig = key[r, :].astype(F32) * value[r, :].astype(F32)
        speed = rate[r, :1]
        window = jnp.sqrt(1.0 - jnp.exp(-2.0 * speed)) * jnp.exp(-speed * position)
        envelope[r, :] = window
        ker = filt[r, :] * window
        send1[2 * p] = stacked(sig[:8], ker[:8]).astype(BF16)
        send1[2 * p + 1] = stacked(sig[8:], ker[8:]).astype(BF16)

    loads[4].wait()
    pl.semaphore_wait(barrier, PIECES - 1 + 3)

    def gather_copy(slot, chunk, target):
        begin, count = CHUNKS[chunk]
        rows = gathered.at[pl.ds(pl.multiple_of(blocks * slot + begin, 16), count)]
        return pltpu.make_async_remote_copy(
            src_ref=rows,
            dst_ref=rows,
            send_sem=ag_send,
            recv_sem=ag_recv.at[slot, chunk],
            device_id={"chan": target},
            device_id_type=MESH,
        )

    span = range(len(CHUNKS))
    middle = len(CHUNKS) // 2
    above_far = above + 1 - 2 * (above % 2)
    below_far = below + 1 - 2 * (below % 2)

    def relay(from_below, from_above, chunk):
        if chunk < middle:
            return gather_copy(from_below, chunk, above)
        return gather_copy(from_above, chunk, below)

    def to_owners(source, landing, send_sem, recv_sem):
        @pl.loop(1, PIECES)
        def _(k):
            target = (me + k) % PIECES

            @pl.when(target < owners)
            def _():
                go(exchange(me, target, source, landing, send_sem, recv_sem))

        @pl.when(owner)
        def _():
            landing[me] = source[me]

    def pass_far(c):
        land(gather_copy(far, c, far))
        go(gather_copy(far, c, above))
        go(gather_copy(far, c, below))

    for c in span[:FLIGHT]:
        go(gather_copy(group, c, far))
    for c in span:
        go(gather_copy(group, c, above))
        go(gather_copy(group, (c + middle) % len(CHUNKS), below))
    for load in loads[5:]:
        load.wait()
    first[...] = first_in[...].astype(BF16)
    for i, part in enumerate((0, 1, 0)):
        rows = pl.ds(2 * SIDE * i, 2 * SIDE)
        forward[rows, :] = forward_in[part].astype(BF16)
        backward[rows, :] = backward_in[part].astype(BF16)
        last[:, rows] = last_in[part].astype(BF16)
    if A1POS == 0:
        to_owners(send1, recv1, ss1, rs1)
    for c in span:
        pass_far(c)
        if c + FLIGHT < len(CHUNKS):
            go(gather_copy(group, c + FLIGHT, far))
        if c + 1 == A1POS:
            to_owners(send1, recv1, ss1, rs1)
        if c + 1 == OWNPOS:
            for d in span:
                land(relay(below, above, d))
                go(relay(below, above, d))
    for c in span:
        land(relay(below_far, above_far, c))
        go(relay(below_far, above_far, c))

    @pl.when(owner)
    def _():
        land(all_of(PIECES - 1, sibling, send1, recv1, ss1, rs1))

        @pl.loop(0, PIECES, unroll=4)
        def _(s):
            piece = recv1[s].astype(F32)
            for i in range(4):
                rows1[pl.ds(pl.multiple_of((s * 4 + i) * 16, 16), 16), :] = piece[:, i * SIDE : (i + 1) * SIDE]

        @pl.loop(0, OWNED // BATCH)
        def _(b):
            cs = [b * BATCH + i for i in range(BATCH)]
            sig = [rows1[pl.ds(c, SIDE, stride=16), :].astype(BF16) for c in cs]
            ker = [rows1[pl.ds(c + 8, SIDE, stride=16), :].astype(BF16) for c in cs]
            spec = forward_pair(jnp.concatenate(sig + ker, 1), first, twist, forward, 2 * BATCH)
            specs[b] = spec
            y = backward_pair(
                product(spec[: SIDE * BATCH], spec[SIDE * BATCH :]), twist, backward, last, BATCH
            )
            for i in range(BATCH):
                out1[pl.ds(i, SIDE, stride=BATCH), :] = y[:, i * SIDE : (i + 1) * SIDE]

            @pl.loop(0, PIECES, unroll=4)
            def _(s):
                send3[b, s] = out1[pl.ds(pl.multiple_of(s * 16, 16), 16), :].astype(BF16)

            @pl.loop(1, PIECES)
            def _(k):
                go(exchange(me, (me + k) % PIECES, send3.at[b], recv3.at[b], ss3.at[b], rs3.at[b]))

            recv3[b, me] = send3[b, me]

    for c in span:
        if c < middle:
            land(gather_copy(above, c, above))
            land(gather_copy(above_far, c, above))
        else:
            land(gather_copy(below, c, below))
            land(gather_copy(below_far, c, below))
        opposite = (group + 4) % GROUPS
        land(gather_copy(opposite, c, above))
        land(gather_copy(opposite + 1 - 2 * (opposite % 2), c, above))
    depth = blocks * GROUPS
    for n in range(length // HALF):
        cols = pl.ds(n * HALF, HALF)
        upstream[:, cols] = dot(weight[...], gathered[pl.ds(0, depth), cols])

    @pl.loop(0, pairs)
    def _(p):
        r = pl.ds(pl.multiple_of(16 * p, 16), 16)
        g = upstream[r, :] * gate[r, :].astype(F32)
        for o in range(2):
            for b in range(2):
                q = g[8 * o + 4 * b : 8 * o + 4 * b + 4]
                quarters = [q[:, i * SIDE : (i + 1) * SIDE] for i in range(4)]
                send2[b, 2 * p + o] = jnp.concatenate(quarters, 0).astype(BF16)

    for b in range(2):
        to_owners(send2.at[b], recv2.at[b], ss2.at[b], rs2.at[b])

    def from_owners(source, landing, send_sem, recv_sem):
        @pl.when(owner)
        def _():
            land(all_of(owners - 1, sibling, source, landing, send_sem, recv_sem))

        @pl.when(me >= owners)
        def _():
            land(all_of(owners, sibling, source, landing, send_sem, recv_sem))

    for b in range(2):
        from_owners(send3.at[b], recv3.at[b], ss3.at[b], rs3.at[b])

    @pl.loop(0, pairs)
    def _(p):
        r = pl.ds(pl.multiple_of(16 * p, 16), 16)
        parts = []
        for o in range(2):
            for b in range(2):
                a = recv3[b, 2 * p + o].astype(F32)
                parts.append(jnp.concatenate([a[4 * i : 4 * i + 4] for i in range(4)], 1))
        conv = jnp.concatenate(parts, 0)
        gate_grad[r, :] = (upstream[r, :] * conv).astype(BF16)
        high, low = split(gate[r, :].astype(F32) * conv)
        gated[r, :] = beside(high, low)

    for t in range(THIRDS):
        third(gate_grad, gate_grad_hbm, out_sem, 0, t).start()

    for j in range(GROUPS):
        rows = gathered[pl.ds(blocks * j, HALF), :]
        term = lax.dot_general(
            beside(rows, rows), gated[...], (((1,), (1,)), ((), ())), preferred_element_type=F32
        )
        for g in range(4):
            partial[g % 2, 2 * j + g // 2] = term[60 * g : 60 * g + 64]

    core_copy = pltpu.make_async_remote_copy(
        src_ref=partial.at[1 - core],
        dst_ref=core_in,
        send_sem=core_send,
        recv_sem=core_recv,
        device_id={"seq": sibling},
        device_id_type=MESH,
    )
    go(core_copy)

    def x_copy(k):
        there = (x + k) % 4
        return pltpu.make_async_remote_copy(
            src_ref=chip_sum.at[pl.ds(4 * there, 4)],
            dst_ref=x_in.at[k - 1],
            send_sem=x_send.at[k - 1],
            recv_sem=x_recv.at[k - 1],
            device_id={"seq": (me + 8 * k) % PIECES},
            device_id_type=MESH,
        )

    land(core_copy)
    partial[core] = partial[core] + core_in[...]
    chip_sum[...] = partial[core].astype(BF16)
    for k in (1, 2, 3):
        go(x_copy(k))

    def correlate(b):
        @pl.when(owner)
        def _():
            land(all_of(PIECES - 1, sibling, send2.at[b], recv2.at[b], ss2.at[b], rs2.at[b]))

            @pl.loop(0, PIECES, unroll=4)
            def _(s):
                rows2[pl.ds(pl.multiple_of(s * 16, 16), 16), :] = recv2[b, s].astype(F32)

            g = [rows2[pl.ds(i, SIDE, stride=BATCH), :].astype(BF16) for i in range(BATCH)]
            gspec = forward_pair(jnp.concatenate(g, 1), first, twist, forward, BATCH)
            spec = specs[b]
            both = stacked(
                product_conj(spec[SIDE * BATCH :], gspec), product_conj(spec[: SIDE * BATCH], gspec)
            )
            y = backward_pair(both, twist, backward, last, 2 * BATCH)
            for i in range(2 * BATCH):
                out2[pl.ds(i, SIDE, stride=8), :] = y[:, i * SIDE : (i + 1) * SIDE]

            @pl.loop(0, PIECES, unroll=4)
            def _(s):
                t = [out2[pl.ds(pl.multiple_of((s * 4 + i) * 8, 8), 8), :] for i in range(4)]
                send4[b, s] = beside(stacked(t[0], t[2]), stacked(t[1], t[3])).astype(BF16)

            @pl.loop(1, PIECES)
            def _(k):
                go(exchange(me, (me + k) % PIECES, send4.at[b], recv4.at[b], ss4.at[b], rs4.at[b]))

            recv4[b, me] = send4[b, me]

    correlate(0)

    correlate(1)

    for k in (1, 2, 3):
        land(x_copy(k))
    x_sum[...] = partial[core, pl.ds(4 * x, 4)] + x_in[0].astype(F32) + x_in[1].astype(F32) + x_in[2].astype(F32)

    def z_copy(k):
        there = (z + k) % 4
        return pltpu.make_async_remote_copy(
            src_ref=x_out.at[there],
            dst_ref=z_in.at[k - 1],
            send_sem=z_send.at[k - 1],
            recv_sem=z_recv.at[k - 1],
            device_id={"seq": x * 8 + there * 2 + core},
            device_id_type=MESH,
        )

    x_out[...] = x_sum[...].astype(BF16)
    for k in (1, 2, 3):
        go(z_copy(k))

    for b in range(2):
        from_owners(send4.at[b], recv4.at[b], ss4.at[b], rs4.at[b])

    outs = ((key_grad, key_grad_hbm), (value_grad, value_grad_hbm), (filter_grad, filter_grad_hbm))
    for t in range(THIRDS):
        @pl.loop(t * pairs // THIRDS, (t + 1) * pairs // THIRDS)
        def _(p):
            r = pl.ds(pl.multiple_of(16 * p, 16), 16)
            parts = []
            for o in range(2):
                for b in range(2):
                    a = recv4[b, 2 * p + o].astype(F32)
                    parts.append(beside(a[:8], a[8:]))
            sgrad = jnp.concatenate([a[:4] for a in parts], 0)
            kgrad = jnp.concatenate([a[4:] for a in parts], 0)
            key_grad[r, :] = (sgrad * value[r, :].astype(F32)).astype(BF16)
            value_grad[r, :] = (sgrad * key[r, :].astype(F32)).astype(BF16)
            filter_grad[r, :] = kgrad * envelope[r, :]

        for n, (source, target) in enumerate(outs):
            third(source, target, out_sem, 1 + n, t).start()

    for k in (1, 2, 3):
        land(z_copy(k))
    total = x_sum[z] + z_in[0].astype(F32) + z_in[1].astype(F32) + z_in[2].astype(F32)
    weight_grad[...] = total[: weight_grad.shape[0], :blocks]
    weight_out = pltpu.make_async_copy(weight_grad, weight_grad_hbm, out_sem.at[4, 0])
    weight_out.start()

    for k in (1, 2, 3):
        leave(x_copy(k))
        leave(z_copy(k))
    leave(core_copy)
    sent = gathered.at[pl.ds(0, 7 * blocks)]
    leave(
        pltpu.make_async_remote_copy(
            src_ref=sent,
            dst_ref=sent,
            send_sem=ag_send,
            recv_sem=ag_recv.at[0, 0],
            device_id={"chan": far},
            device_id_type=MESH,
        )
    )

    @pl.when(owner)
    def _():
        leave(all_of(owners - 1, sibling, send1, recv1, ss1, rs1))
        for b in range(2):
            leave(all_of(owners - 1, sibling, send2.at[b], recv2.at[b], ss2.at[b], rs2.at[b]))
            leave(all_of(PIECES - 1, sibling, send3.at[b], recv3.at[b], ss3.at[b], rs3.at[b]))
            leave(all_of(PIECES - 1, sibling, send4.at[b], recv4.at[b], ss4.at[b], rs4.at[b]))

    @pl.when(me >= owners)
    def _():
        leave(all_of(owners, sibling, send1, recv1, ss1, rs1))
        for b in range(2):
            leave(all_of(owners, sibling, send2.at[b], recv2.at[b], ss2.at[b], rs2.at[b]))

    for t in range(THIRDS):
        third(gate_grad, gate_grad_hbm, out_sem, 0, t).wait()
        for n, (source, target) in enumerate(outs):
            third(source, target, out_sem, 1 + n, t).wait()
    weight_out.wait()


def settle_kernel(*refs):
    count = len(refs) // 3
    inward, outward = [], []
    for i in range(count):
        for t in range(THIRDS):
            inward.append(third(refs[i], refs[2 * count + i], refs[-2], i, t))
            outward.append(third(refs[2 * count + i], refs[count + i], refs[-1], i, t))
    for copy in inward:
        copy.start()
    for copy, onward in zip(inward, outward):
        copy.wait()
        onward.start()
    for onward in outward:
        onward.wait()


def per_device(gate_act, key_act, value_act, filter_raw, decay_rate, out_weight, out_grad):
    channels, length = gate_act.shape
    tables = [jnp.asarray(t) for t in make_tables()]
    shape = (channels, length)
    vmem = pltpu.VMEM
    dma = pltpu.SemaphoreType.DMA
    rows = SIDE * OWNED
    results = pl.pallas_call(
        whole_kernel,
        out_shape=(
            jax.ShapeDtypeStruct(shape, BF16),
            jax.ShapeDtypeStruct(shape, BF16),
            jax.ShapeDtypeStruct(shape, BF16),
            jax.ShapeDtypeStruct(shape, F32),
            jax.ShapeDtypeStruct((channels * GROUPS // PIECES, channels), F32),
        ),
        in_specs=[pl.BlockSpec(memory_space=pltpu.HBM)] * 12,
        out_specs=(pl.BlockSpec(memory_space=pltpu.HBM),) * 5,
        scratch_shapes=[
            vmem(shape, BF16),
            vmem(shape, BF16),
            vmem(shape, BF16),
            vmem(shape, F32),
            vmem((channels * GROUPS // PIECES, channels), F32),
            dma((5, THIRDS)),
            vmem(shape, BF16),
            vmem(shape, BF16),
            vmem(shape, BF16),
            vmem(shape, F32),
            vmem((1, channels), F32),
            vmem((2 * SIDE, SIDE), F32),
            vmem(out_weight.shape, BF16),
        ]
        + [vmem(t.shape, t.dtype) for t in tables]
        + [
            vmem((2 * SIDE, 2 * SIDE), BF16),
            vmem((6 * SIDE, 2 * SIDE), BF16),
            vmem((6 * SIDE, 2 * SIDE), BF16),
            vmem((SIDE, 6 * SIDE), BF16),
            vmem((PIECES, 16, length), BF16),
            vmem((PIECES, 16, length), BF16),
            vmem((2, PIECES, 16, SIDE), BF16),
            vmem((2, PIECES, 16, SIDE), BF16),
            vmem((2, PIECES, 16, SIDE), BF16),
            vmem((2, PIECES, 16, SIDE), BF16),
            vmem((2, PIECES, 16, HALF), BF16),
            vmem((2, PIECES, 16, HALF), BF16),
            vmem((channels * GROUPS + 16, length), BF16),
            vmem(shape, F32),
            vmem(shape, F32),
            vmem((2 * rows, SIDE), F32),
            vmem((SIDE * BATCH, SIDE), F32),
            vmem((OWNED // BATCH, 2 * SIDE * BATCH, 2 * SIDE), F32),
            vmem((SIDE * BATCH, SIDE), F32),
            vmem((rows, SIDE), F32),
            vmem((channels + 16, 2 * length), BF16),
            vmem((2, 16, 64, HALF), F32),
            vmem((16, 64, HALF), F32),
            vmem((16, 64, HALF), BF16),
            vmem((3, 4, 64, HALF), BF16),
            vmem((4, 64, HALF), F32),
            vmem((4, 64, HALF), BF16),
            vmem((3, 64, HALF), BF16),
            dma((12,)),
        ]
        + [dma] * 2
        + [dma((2,))] * 6
        + [dma, dma((GROUPS, len(CHUNKS))), dma, dma]
        + [dma((3,))] * 4,
        compiler_params=pltpu.CompilerParams(
            collective_id=0, has_side_effects=True, vmem_limit_bytes=LIMIT
        ),
    )(gate_act, key_act, value_act, filter_raw, decay_rate[None, :], out_weight, out_grad, *tables)
    *grads, weight_grad = pl.pallas_call(
        settle_kernel,
        out_shape=tuple(jax.ShapeDtypeStruct(r.shape, r.dtype) for r in results),
        in_specs=[pl.BlockSpec(memory_space=pltpu.HBM)] * 5,
        out_specs=[pl.BlockSpec(memory_space=pltpu.HBM)] * 5,
        scratch_shapes=[vmem(r.shape, r.dtype) for r in results] + [dma((5, THIRDS))] * 2,
        compiler_params=pltpu.CompilerParams(vmem_limit_bytes=LIMIT),
    )(*results)
    return (*grads, weight_grad.T)


def solution(mesh):
    rows = P("chan", "seq")
    return jax.shard_map(
        per_device,
        mesh=mesh,
        in_specs=(rows, rows, rows, rows, P("chan"), P("chan", None), rows),
        out_specs=(rows,) * 5,
        check_vma=False,
    )
```
